32 devices in a mesh: groups: 2 (over y), seq: 4 (over z), head: 2 (over x), rep: 2 (over core).
Axes of the slice: x: 2, y: 2, z: 4, core: 2. Of those that a mesh axis runs over, the one named last changes fastest.
Arguments:
- queries: bfloat16 [32768, 16, 128], P(('groups', 'seq'), ('head', 'rep')), parts along dimension 0, may hold values from -8 to 8
- keys: bfloat16 [32768, 128], P(('groups', 'seq')), parts along dimension 0, may hold values from -6 to 6
- values: bfloat16 [32768, 128], P(('groups', 'seq')), parts along dimension 0, may hold values from -6 to 6
- query_maps: bfloat16 [32, 128, 128], P(('groups', 'head', 'rep')), parts along dimension 0, may hold values from -0.5 to 0.5
- key_map: bfloat16 [256, 128], P('groups'), parts along dimension 0, may hold values from -0.046875 to 0.046875
- linear_cotangent: bfloat16 [32768, 16, 128], P(('groups', 'seq'), ('head', 'rep')), parts along dimension 0, may hold values from -0.046875 to 0.046875
Outputs:
- softmax_out: bfloat16 [32768, 16, 128], P(('groups', 'seq'), ('head', 'rep')), parts along dimension 0
- linear_out: bfloat16 [32768, 16, 128], P(('groups', 'seq'), ('head', 'rep')), parts along dimension 0
- map_gradient: float32 [256, 16, 128], P(('groups', 'seq'), ('head', 'rep')), parts along dimension 0
The draws below stay inside these ranges and needn't reach their ends.
There are 2 independent parts, one for each index of `groups`. The reference program is written for one: setup_inputs(seed, part) draws one part's arguments, and reference() takes and returns one part's arrays. A program takes and returns all parts, laid end to end along the dimension named above; each array names one. Nothing has to cross between parts.
All inputs are finite; a program needn't handle non-finite values.
Results may differ from the reference program's by a relative error of at most 0.0058.
Values may be sent and summed in bfloat16 or wider, within the bound.
No kernel may reach another device: no remote copies, remote signals or barrier semaphores. Data moves between devices by JAX's collectives and lax.ppermute only.
A program may use at most 128 MiB of HBM per device.

```python
import jax
import jax.numpy as jnp
from jax import lax

H = 16
HD = 128
W = 512
TOKENS = 16384


def draw_keys(key, part):
    drawn = jnp.clip(jax.random.normal(jax.random.fold_in(key, 11), (TOKENS, HD), jnp.float32), -6.0, 6.0)
    return drawn.astype(jnp.bfloat16)


def draw_queries(key, part):
    drawn = jnp.clip(jax.random.normal(jax.random.fold_in(key, 21), (TOKENS, H, HD), jnp.float32), -6.0, 6.0)
    return drawn.astype(jnp.bfloat16)


def block_scale(own_key, extent, cuts, least, largest):
    gain, own = 1.0, jax.random.fold_in(own_key, 6)
    for position, blocks in cuts:
        draws = jnp.exp(jax.random.uniform(jax.random.fold_in(own, position), (blocks,), jnp.float32, least / len(cuts), largest / len(cuts)))
        gain = gain * jnp.repeat(draws, extent[position] // blocks).reshape([-1 if axis == position else 1 for axis in range(len(extent))])
    return gain


def normal_values(own_key, shape, scale, most, cuts=(), kind=jnp.bfloat16):
    values = scale * jax.random.normal(own_key, shape, jnp.float32)
    if cuts:
        values = values * block_scale(own_key, shape, cuts, -0.22, 0.18)
    return jnp.clip(values, -most, most).astype(kind)


def setup_inputs(seed: int = 0, part: int = 0) -> dict:
    arg_keys = jax.random.split(jax.random.key(seed), 7)
    part_splits = jax.random.split(jax.random.fold_in(arg_keys[6], part), 7)
    queries = draw_queries(jax.random.fold_in(jax.random.fold_in(arg_keys[6], part), 71), part)
    keys = draw_keys(jax.random.fold_in(jax.random.fold_in(arg_keys[6], part), 71), part)
    values = normal_values(part_splits[2], (TOKENS, HD), 1.0, 6.0, ((0, 4),))
    query_maps = normal_values(part_splits[3], (H, HD, HD), HD ** -0.5, 0.5, ((0, 4),))
    key_map = normal_values(part_splits[4], (HD, HD), (HD * HD) ** -0.5, 0.046875)
    linear_cotangent = normal_values(part_splits[5], (TOKENS, H, HD), (1.0 / TOKENS ** 0.5), 0.046875, ((0, 4), (1, 4)))
    return {"queries": queries, "keys": keys, "values": values, "query_maps": query_maps, "key_map": key_map, "linear_cotangent": linear_cotangent}


def window_block(block_index, start_state, tensors):
    queries, keys_ext, values_ext, query_features, key_features, values, cotangent = tensors
    highest_precision = lax.Precision.HIGHEST
    first_row = block_index * W
    head_dim = keys_ext.shape[1]
    query_block = lax.dynamic_slice_in_dim(queries, first_row, W, 0).astype(jnp.float32)
    key_window = lax.dynamic_slice_in_dim(keys_ext, first_row, 2 * W, 0).astype(jnp.float32)
    value_window = lax.dynamic_slice_in_dim(values_ext, first_row, 2 * W, 0).astype(jnp.float32)
    query_pos = first_row + jnp.arange(W, dtype=jnp.int32)
    key_pos = first_row - W + jnp.arange(2 * W, dtype=jnp.int32)
    spacing = query_pos[:, None] - key_pos[None, :]
    allowed = (spacing >= 0) & (spacing < W) & (key_pos[None, :] >= 0)
    scores = jnp.einsum('whd,kd->hwk', query_block, key_window, precision=highest_precision) * head_dim ** (-0.5)
    scores = jnp.where(allowed[None], scores, -1e+30)
    highest = lax.optimization_barrier(jnp.max(scores, axis=2, keepdims=True))
    shifted_exp = jnp.exp(scores - highest)
    weights = (shifted_exp / lax.optimization_barrier(jnp.sum(shifted_exp, axis=2, keepdims=True))).astype(jnp.bfloat16)
    soft_block = jnp.einsum('hwk,kd->whd', weights.astype(jnp.float32), value_window, precision=highest_precision).astype(jnp.bfloat16)
    feature_block = lax.dynamic_slice_in_dim(query_features, first_row, W, 0).astype(jnp.float32)
    key_block = lax.dynamic_slice_in_dim(key_features, first_row, W, 0).astype(jnp.float32)
    value_block = lax.dynamic_slice_in_dim(values, first_row, W, 0).astype(jnp.float32)
    cotangent_block = lax.dynamic_slice_in_dim(cotangent, first_row, W, 0).astype(jnp.float32)
    causal = jnp.arange(W)[:, None] >= jnp.arange(W)[None, :]
    factor = lax.rsqrt((query_pos + 1).astype(jnp.float32))[:, None, None]
    linear_scores = jnp.where(causal[None], jnp.einsum('whf,sf->hws', feature_block, key_block, precision=highest_precision), 0.0).astype(jnp.bfloat16)
    inside = jnp.einsum('hws,sd->whd', linear_scores.astype(jnp.float32), value_block, precision=highest_precision)
    carried = jnp.einsum('whf,fd->whd', feature_block, start_state, precision=highest_precision)
    linear_block = (factor * (inside + carried)).astype(jnp.bfloat16)
    back_scores = jnp.where(causal[None], jnp.einsum('whd,sd->hws', cotangent_block, value_block, precision=highest_precision), 0.0).astype(jnp.bfloat16)
    back_inside = jnp.einsum('hws,sf->whf', back_scores.astype(jnp.float32), key_block, precision=highest_precision)
    back_carried = jnp.einsum('whd,fd->whf', cotangent_block, start_state, precision=highest_precision)
    feature_gradient = (factor * (back_inside + back_carried)).astype(jnp.bfloat16)
    return (soft_block, linear_block, feature_gradient)

def reference(queries, keys, values, query_maps, key_map, linear_cotangent):
    token_count = keys.shape[0]
    head_dim = keys.shape[1]
    head_count = queries.shape[1]
    block_count = token_count // W
    key_features = jnp.dot(keys, key_map, preferred_element_type=jnp.float32).astype(jnp.bfloat16)
    query_features = jnp.einsum('thd,hdf->thf', queries.astype(jnp.float32), query_maps.astype(jnp.float32), precision=lax.Precision.HIGHEST).astype(jnp.bfloat16)
    block_states = jnp.einsum('bwf,bwd->bfd', key_features.reshape(block_count, W, head_dim).astype(jnp.float32), values.reshape(block_count, W, head_dim).astype(jnp.float32), precision=lax.Precision.HIGHEST)
    running = jnp.cumsum(block_states, axis=0)
    starts = jnp.concatenate([jnp.zeros_like(block_states[:1]), running[:-1]], axis=0)
    padding = jnp.zeros((W, head_dim), keys.dtype)
    keys_ext = jnp.concatenate([padding, keys], axis=0)
    values_ext = jnp.concatenate([padding, values], axis=0)
    tensors = (queries, keys_ext, values_ext, query_features, key_features, values, linear_cotangent)

    def one_block(block_item):
        return window_block(block_item[0], block_item[1], tensors)
    soft_parts, linear_parts, gradient_parts = lax.map(one_block, (jnp.arange(block_count, dtype=jnp.int32), starts))
    softmax_out = soft_parts.reshape(token_count, head_count, head_dim)
    linear_out = linear_parts.reshape(token_count, head_count, head_dim)
    feature_gradient = gradient_parts.reshape(token_count, head_count, head_dim)
    map_gradient = jnp.einsum('the,thf->ehf', queries.astype(jnp.float32), feature_gradient.astype(jnp.float32), precision=lax.Precision.HIGHEST)
    return (softmax_out, linear_out, map_gradient)
```

```python
import functools

import jax
import jax.numpy as jnp
import numpy as np
from jax import lax
from jax.experimental import pallas as pl
from jax.experimental.pallas import tpu as pltpu
from jax.sharding import PartitionSpec as P

W = 512
TILE = 128
BF = jnp.bfloat16
F32 = jnp.float32
LOG2E = 1.4426950408889634
VMEM_LIMIT = 56 * 2**20


def dot_nn(a, b):
    return jnp.dot(a, b, preferred_element_type=F32)


def dot_nt(a, b):
    return lax.dot_general(a, b, (((1,), (1,)), ((), ())), preferred_element_type=F32)


def dot_tn(a, b):
    return lax.dot_general(a, b, (((0,), (0,)), ((), ())), preferred_element_type=F32)


def tokens_of_rows(rows, heads):
    return lax.broadcasted_iota(jnp.int32, (rows, TILE), 0) // heads


def padded16(rows):
    return -(-rows // 16) * 16


def backward_kernel(
    heads, ranks, slab, q_ref, c_ref, k_ref, v_ref, map_ref, send_ref, rim_ref, acc, state, qs, cs, fs, gi, qi
):
    step, steps = pl.program_id(0), pl.num_programs(0)
    head_dim = map_ref.shape[0]
    tiles = k_ref.shape[0] // TILE
    rows = TILE * heads

    @pl.when(step == 0)
    def _():
        acc[...] = jnp.zeros_like(acc)
        state[...] = jnp.zeros_like(state)

    first = lax.axis_index("seq") * (steps * tiles * TILE) + step * (tiles * TILE)
    tok = tokens_of_rows(rows, heads)
    causal = lax.broadcasted_iota(jnp.int32, (rows, TILE), 1) <= tok
    key_features = dot_nn(k_ref[...], map_ref[...]).astype(BF)
    carried = state[...]
    for t in range(tiles):
        sl, tl = slice(t * rows, (t + 1) * rows), slice(t * TILE, (t + 1) * TILE)
        cot, val, kf = c_ref[sl, :], v_ref[tl, :], key_features[tl, :]
        back = jnp.where(causal, dot_nt(cot, val), 0.0).astype(BF)
        fs[sl, :] = dot_nn(
            jnp.concatenate([back, cot], 1), jnp.concatenate([kf, carried.astype(BF)], 0)
        )
        factor = lax.rsqrt((tok + (first + t * TILE + 1)).astype(F32))
        qs[sl, :] = q_ref[sl, :].astype(F32) * factor
        cs[sl, :] = cot.astype(F32)
        carried = carried + dot_tn(val, kf)
    state[...] = carried
    for h in range(heads):
        pick = pl.ds(h, tiles * TILE, stride=heads)
        right = jnp.concatenate([fs[pick, :].astype(BF), cs[pick, :].astype(BF)], 1)
        acc[h] += dot_tn(qs[pick, :].astype(BF), right)

    @pl.when(step == steps - 1)
    def _():
        for h in range(heads):
            pick = pl.ds(h, head_dim, stride=heads)
            gi[pick, :] = acc[h, :, :head_dim]
            qi[pick, :] = acc[h, :, head_dim:]
        total = state[...]
        high = total.astype(BF)
        low = (total - high.astype(F32)).astype(BF)
        for d in range(ranks):
            send_ref[d, :head_dim, :] = jnp.concatenate([high, low], 1)
            part = jnp.concatenate(
                [gi[d * slab : (d + 1) * slab, :], qi[d * slab : (d + 1) * slab, :]], 1
            )
            spare = padded16(slab) - slab
            if spare:
                part = jnp.concatenate([part, jnp.zeros((spare, 2 * head_dim), F32)], 0)
            send_ref[d, head_dim:, :] = part.astype(BF)
        rim_ref[:W, :] = k_ref[...][-W:, :]
        rim_ref[W:, :] = v_ref[...][-W:, :]


def soft_block(heads, q_ref, keys_before, keys_here, values_before, values_here, o_ref, before_ok):
    head_dim = q_ref.shape[1]
    scale = float(LOG2E / np.sqrt(head_dim))
    rows = TILE * heads
    low = lax.broadcasted_iota(jnp.int32, (rows, TILE), 1) <= tokens_of_rows(rows, heads)
    for t in range(W // TILE):
        sl = slice(t * rows, (t + 1) * rows)
        start, end = t * TILE, (t + 1) * TILE
        keys = jnp.concatenate([keys_before[start:, :], keys_here[:end, :]], 0)
        values = jnp.concatenate([values_before[start:, :], values_here[:end, :]], 0)
        scores = dot_nt(q_ref[sl, :], keys)
        parts = [scores[:, j * TILE : (j + 1) * TILE] for j in range(W // TILE + 1)]
        parts[0] = jnp.where(low, -1e30, parts[0])
        parts[-1] = jnp.where(low, parts[-1], -1e30)
        if before_ok is not None:
            for j in range(W // TILE - t):
                parts[j] = jnp.where(before_ok, parts[j], -1e30)
        highest = jnp.max(functools.reduce(jnp.maximum, parts), axis=1, keepdims=True)
        weights = jnp.concatenate(
            [jnp.exp2((part - highest) * scale).astype(BF) for part in parts], 1
        )
        both = dot_nn(weights, jnp.concatenate([values, jnp.ones_like(values)], 1))
        o_ref[sl, :] = (both[:, :head_dim] / both[:, head_dim:]).astype(BF)


def softmax_kernel(heads, q_ref, kb_ref, kh_ref, vb_ref, vh_ref, o_ref):
    soft_block(heads, q_ref, kb_ref, kh_ref, vb_ref, vh_ref, o_ref, None)


def forward_kernel(
    heads, ranks, slab, q_ref, k_ref, v_ref, map_ref, qmap_ref, got_ref, rim_ref, _, o_ref, soft_ref, grad_ref, state, qs, os
):
    step, steps = pl.program_id(0), pl.num_programs(0)
    head_dim = map_ref.shape[0]
    tiles = k_ref.shape[0] // TILE
    rows = TILE * heads
    rank = lax.axis_index("seq")

    @pl.when(step == 0)
    def _():
        before = jnp.zeros((head_dim, head_dim), F32)
        mine = before
        grad = jnp.zeros((slab, head_dim), F32)
        for r in range(ranks):
            mine = jnp.where(rank == r, before, mine)
            part = got_ref[r, head_dim:, :][:slab]
            if r:
                high = before.astype(BF)
                low = (before - high.astype(F32)).astype(BF)
                grad = grad + dot_nn(part[:, head_dim:], high) + dot_nn(part[:, head_dim:], low)
            grad = grad + part[:, :head_dim].astype(F32)
            states = got_ref[r, :head_dim, :].astype(F32)
            before = before + (states[:, :head_dim] + states[:, head_dim:])
        grad_ref[...] = grad
        state[...] = mine.T
        soft_block(
            heads, q_ref, rim_ref.at[:W], k_ref, rim_ref.at[W:], v_ref, soft_ref, rank > 0
        )

    first = rank * (steps * tiles * TILE) + step * (tiles * TILE)
    qs[...] = q_ref[...].astype(F32)
    key_features = dot_nn(k_ref[...], map_ref[...]).astype(BF)
    features = [
        dot_nn(qs[pl.ds(h, tiles * TILE, stride=heads), :].astype(BF), qmap_ref[h]).astype(BF)
        for h in range(heads)
    ]
    tok = lax.broadcasted_iota(jnp.int32, (TILE, TILE), 0)
    causal = jnp.concatenate([lax.broadcasted_iota(jnp.int32, (TILE, TILE), 1) <= tok] * heads, 0)
    carried = state[...]
    for t in range(tiles):
        tl = slice(t * TILE, (t + 1) * TILE)
        val, kf = v_ref[tl, :], key_features[tl, :]
        qf = jnp.concatenate([x[tl, :] for x in features], 0)
        inner = jnp.where(causal, dot_nt(qf, kf), 0.0).astype(BF)
        out = dot_nn(
            jnp.concatenate([inner, qf], 1), jnp.concatenate([val, carried.astype(BF)], 0)
        )
        factor = lax.rsqrt((tok + (first + t * TILE + 1)).astype(F32))
        for h in range(heads):
            os[pl.ds(t * rows + h, TILE, stride=heads), :] = out[h * TILE : (h + 1) * TILE, :] * factor
        carried = carried + dot_tn(kf, val)
    state[...] = carried
    o_ref[...] = os[...].astype(BF)


def per_device(ranks, queries, keys, values, query_maps, key_map, linear_cotangent):
    tokens, heads, head_dim = queries.shape
    blocks = tokens // W
    block_rows = W * heads
    slab = head_dim // ranks * heads
    params = pltpu.CompilerParams(vmem_limit_bytes=VMEM_LIMIT)
    q_rows = queries.reshape(tokens * heads, head_dim)
    c_rows = linear_cotangent.reshape(tokens * heads, head_dim)
    row_spec = pl.BlockSpec((block_rows, head_dim), lambda i: (i, 0))
    key_spec = pl.BlockSpec((W, head_dim), lambda i: (i, 0))

    def whole(shape):
        return pl.BlockSpec(shape, lambda i: (0,) * len(shape))

    packet = (ranks, head_dim + padded16(slab), 2 * head_dim)
    send, rim = pl.pallas_call(
        functools.partial(backward_kernel, heads, ranks, slab),
        grid=(blocks,),
        in_specs=[row_spec, row_spec, key_spec, key_spec, whole(key_map.shape)],
        out_specs=[whole(packet), whole((2 * W, head_dim))],
        out_shape=[
            jax.ShapeDtypeStruct(packet, BF),
            jax.ShapeDtypeStruct((2 * W, head_dim), BF),
        ],
        scratch_shapes=[
            pltpu.VMEM((heads, head_dim, 2 * head_dim), F32),
            pltpu.VMEM((head_dim, head_dim), F32),
            pltpu.VMEM((block_rows, head_dim), F32),
            pltpu.VMEM((block_rows, head_dim), F32),
            pltpu.VMEM((block_rows, head_dim), F32),
            pltpu.VMEM((heads * head_dim, head_dim), F32),
            pltpu.VMEM((heads * head_dim, head_dim), F32),
        ],
        compiler_params=params,
        name="backward",
    )(q_rows, c_rows, keys, values, key_map)

    got = lax.all_to_all(send, "seq", 0, 0)
    rim = lax.ppermute(rim, "seq", [(r, r + 1) for r in range(ranks - 1)])

    later_rows = pl.BlockSpec((block_rows, head_dim), lambda i: (i + 1, 0))
    later_keys = pl.BlockSpec((W, head_dim), lambda i: (i + 1, 0))
    soft_rows = pl.pallas_call(
        functools.partial(softmax_kernel, heads),
        grid=(blocks - 1,),
        in_specs=[later_rows, key_spec, later_keys, key_spec, later_keys],
        out_specs=later_rows,
        out_shape=jax.ShapeDtypeStruct(q_rows.shape, BF),
        compiler_params=params,
        name="softmax",
    )(q_rows, keys, keys, values, values)

    linear_rows, soft_rows, gradient = pl.pallas_call(
        functools.partial(forward_kernel, heads, ranks, slab),
        grid=(blocks,),
        in_specs=[
            row_spec,
            key_spec,
            key_spec,
            whole(key_map.shape),
            whole(query_maps.shape),
            whole(packet),
            whole((2 * W, head_dim)),
            pl.BlockSpec(memory_space=pl.ANY),
        ],
        out_specs=[row_spec, whole((block_rows, head_dim)), whole((slab, head_dim))],
        out_shape=[
            jax.ShapeDtypeStruct(q_rows.shape, BF),
            jax.ShapeDtypeStruct(q_rows.shape, BF),
            jax.ShapeDtypeStruct((slab, head_dim), F32),
        ],
        scratch_shapes=[
            pltpu.VMEM((head_dim, head_dim), F32),
            pltpu.VMEM((block_rows, head_dim), F32),
            pltpu.VMEM((block_rows, head_dim), F32),
        ],
        input_output_aliases={7: 1},
        compiler_params=params,
        name="forward",
    )(q_rows, keys, values, key_map, query_maps, got, rim, soft_rows)

    return (
        soft_rows.reshape(queries.shape),
        linear_rows.reshape(queries.shape),
        gradient.reshape(head_dim // ranks, heads, head_dim),
    )


def solution(mesh):
    return jax.shard_map(
        functools.partial(per_device, mesh.shape["seq"]),
        mesh=mesh,
        in_specs=(
            P(("groups", "seq"), ("head", "rep"), None),
            P(("groups", "seq"), None),
            P(("groups", "seq"), None),
            P(("groups", "head", "rep"), None, None),
            P("groups", None),
            P(("groups", "seq"), ("head", "rep"), None),
        ),
        out_specs=(
            P(("groups", "seq"), ("head", "rep"), None),
            P(("groups", "seq"), ("head", "rep"), None),
            P(("groups", "seq"), ("head", "rep"), None),
        ),
        check_vma=False,
    )
```

```python
import functools

import jax
import jax.numpy as jnp
import numpy as np
from jax import lax
from jax.experimental import pallas as pl
from jax.experimental.pallas import tpu as pltpu
from jax.sharding import PartitionSpec as P

W = 512
TILE = 128
CHUNK = 1024
GROUP = 4
BF = jnp.bfloat16
F32 = jnp.float32
LOG2E = 1.4426950408889634
VMEM_LIMIT = 64 * 2**20 - 2**17


def dot_nn(a, b):
    return jnp.dot(a, b, preferred_element_type=F32)


def dot_nt(a, b):
    return lax.dot_general(a, b, (((1,), (1,)), ((), ())), preferred_element_type=F32)


def dot_tn(a, b):
    return lax.dot_general(a, b, (((0,), (0,)), ((), ())), preferred_element_type=F32)


def tokens_of_rows(rows, heads):
    return lax.broadcasted_iota(jnp.int32, (rows, TILE), 0) // heads


def padded16(rows):
    return -(-rows // 16) * 16


def staged(count, *stages):
    for x in range(count + len(stages) - 1):
        for depth in reversed(range(len(stages))):
            if 0 <= x - depth < count:
                stages[depth](x - depth)


def causal_keep(heads):
    tok = lax.broadcasted_iota(jnp.int32, (TILE, TILE), 0)
    causal = lax.broadcasted_iota(jnp.int32, (TILE, TILE), 1) <= tok
    return jnp.concatenate([jnp.where(causal, 1.0, 0.0)] * heads, 0).astype(BF)


def backward_kernel(
    heads, ranks, slab, q_ref, c_ref, k_ref, v_ref, map_ref, send_ref, rim_ref, acc, state, keep, qs, cs, gi, qi
):
    step, steps = pl.program_id(0), pl.num_programs(0)
    head_dim = map_ref.shape[0]
    tiles = k_ref.shape[0] // TILE
    rows = TILE * heads
    group = min(GROUP, tiles)

    @pl.when(step == 0)
    def _():
        acc[...] = jnp.zeros_like(acc)
        state[...] = jnp.zeros_like(state)
        keep[...] = causal_keep(heads)

    first = lax.axis_index("seq") * (steps * tiles * TILE) + step * (tiles * TILE)
    key_features = dot_nn(k_ref[...], map_ref[...]).astype(BF)
    carried = state[...]
    starts, cots, back, grads = [], {}, {}, {}
    for t in range(tiles):
        tl = slice(t * TILE, (t + 1) * TILE)
        starts.append(carried.astype(BF))
        carried = carried + dot_tn(v_ref[tl, :], key_features[tl, :])
    state[...] = carried

    def widen(t):
        sl = slice(t * rows, (t + 1) * rows)
        qs[sl, :] = q_ref[sl, :].astype(F32)
        cs[sl, :] = c_ref[sl, :].astype(F32)

    def part(ref, t, h, count=TILE):
        return ref[pl.ds(t * rows + h, count, stride=heads), :]

    def score(t):
        cots[t] = jnp.concatenate([part(cs, t, h).astype(BF) for h in range(heads)], 0)
        back[t] = dot_nt(cots[t], v_ref[t * TILE : (t + 1) * TILE, :]).astype(BF) * keep[...]

    def gradient(t):
        out = dot_nn(
            jnp.concatenate([back.pop(t), cots[t]], 1),
            jnp.concatenate([key_features[t * TILE : (t + 1) * TILE, :], starts[t]], 0),
        )
        grads[t] = out.astype(BF)

    def gather(t):
        if (t + 1) % group:
            return
        begin = t + 1 - group
        tok = lax.broadcasted_iota(jnp.int32, (group * TILE, head_dim), 0)
        factor = lax.rsqrt((tok + (first + begin * TILE + 1)).astype(F32))
        for h in range(heads):
            hs = slice(h * TILE, (h + 1) * TILE)
            right = jnp.concatenate(
                [
                    jnp.concatenate([grads[u][hs, :], cots[u][hs, :]], 1)
                    for u in range(begin, t + 1)
                ],
                0,
            )
            acc[h] += dot_tn((part(qs, begin, h, group * TILE) * factor).astype(BF), right)

    staged(tiles, widen, score, gradient, gather)

    @pl.when(step == steps - 1)
    def _():
        for h in range(heads):
            pick = pl.ds(h, head_dim, stride=heads)
            gi[pick, :] = acc[h, :, :head_dim]
            qi[pick, :] = acc[h, :, head_dim:]
        for d in range(ranks):
            send_ref[d, :head_dim, :] = state[...].astype(BF)
            for n, terms in enumerate((gi, qi)):
                part = terms[d * slab : (d + 1) * slab, :]
                spare = padded16(slab) - slab
                if spare:
                    part = jnp.concatenate([part, jnp.zeros((spare, head_dim), F32)], 0)
                begin = head_dim + n * padded16(slab)
                send_ref[d, begin : begin + padded16(slab), :] = part.astype(BF)
        rim_ref[:W, :] = k_ref[...][-W:, :]
        rim_ref[W:, :] = v_ref[...][-W:, :]


def window_biases(heads, before, after):
    rows = TILE * heads
    low = lax.broadcasted_iota(jnp.int32, (rows, TILE), 1) <= tokens_of_rows(rows, heads)
    before[...] = jnp.where(low, -1e30, 0.0)
    after[...] = jnp.where(low, 0.0, -1e30)


def soft_stages(rows, q_ref, o_ref, keys_of, values_of, before, after, extra):
    head_dim = q_ref.shape[1]
    scale = float(LOG2E / np.sqrt(head_dim))
    held = {}

    def score(t):
        held[t] = dot_nt(q_ref[t * rows : (t + 1) * rows, :], keys_of(t))

    def weigh(t):
        scores = held[t]
        parts = [scores[:, j * TILE : (j + 1) * TILE] for j in range(W // TILE + 1)]
        parts[0] = parts[0] + before[...]
        parts[-1] = parts[-1] + after[...]
        if extra is not None:
            parts = [part if j == W // TILE else part + extra(t, j) for j, part in enumerate(parts)]
        highest = jnp.max(functools.reduce(jnp.maximum, parts), axis=1, keepdims=True)
        held[t] = jnp.concatenate(
            [jnp.exp2((part - highest) * scale).astype(BF) for part in parts], 1
        )

    def combine(t):
        values = values_of(t)
        both = dot_nn(held.pop(t), jnp.concatenate([values, jnp.ones_like(values)], 1))
        o_ref[t * rows : (t + 1) * rows, :] = (both[:, :head_dim] / both[:, head_dim:]).astype(BF)

    return score, weigh, combine


def softmax_kernel(heads, q_ref, kb_ref, kh_ref, vb_ref, vh_ref, o_ref, before, after):
    @pl.when(pl.program_id(0) == 0)
    def _():
        window_biases(heads, before, after)

    def window(left, here):
        def of(t):
            start, end = t * TILE, (t + 1) * TILE
            if start >= W:
                return here[start - W : end, :]
            return jnp.concatenate([left[start:, :], here[:end, :]], 0)

        return of

    stages = soft_stages(
        TILE * heads, q_ref, o_ref, window(kb_ref, kh_ref), window(vb_ref, vh_ref), before, after, None
    )
    count = kh_ref.shape[0] // TILE
    skipped = W // TILE

    @pl.when(pl.program_id(0) == 0)
    def _():
        if count > skipped:
            staged(count - skipped, *(lambda t, stage=stage: stage(t + skipped) for stage in stages))

    @pl.when(pl.program_id(0) > 0)
    def _():
        staged(count, *stages)


def forward_kernel(
    heads, ranks, slab, soft_steps, q_ref, k_ref, v_ref, map_ref, qmap_ref, soft_q_ref, got, rim_ref, _,
    o_ref, soft_ref, grad_ref, state, keep, qs, os, keys_ext, values_ext, before, after
):
    step, steps = pl.program_id(0), pl.num_programs(0)
    head_dim = map_ref.shape[0]
    tokens = k_ref.shape[0]
    tiles = tokens // TILE
    rows = TILE * heads
    rank = lax.axis_index("seq")

    @pl.when(step == 0)
    def _():
        keys_ext[:W, :] = rim_ref[:W, :]
        values_ext[:W, :] = rim_ref[W:, :]
        keys_ext[W:, :] = k_ref[:W, :]
        values_ext[W:, :] = v_ref[:W, :]
        window_biases(heads, before, after)
        keep[...] = causal_keep(heads)
        earlier = jnp.zeros((head_dim, head_dim), F32)
        mine = earlier
        grad = jnp.zeros((slab, head_dim), F32)
        for r in range(ranks):
            mine = jnp.where(rank == r, earlier, mine)
            middle = head_dim + padded16(slab)
            grad = grad + got[r, head_dim:middle, :].astype(F32)[:slab]
            if r:
                high = earlier.astype(BF)
                low = (earlier - high.astype(F32)).astype(BF)
                products = got[r, middle:, :]
                grad = grad + (dot_nn(products, high) + dot_nn(products, low))[:slab]
            earlier = earlier + got[r, :head_dim, :].astype(F32)
        grad_ref[...] = grad
        state[...] = mine.T

    first = rank * (steps * tokens) + step * tokens
    soft_tiles = soft_q_ref.shape[0] // rows
    soft_first = jnp.minimum(step, soft_steps - 1) * soft_tiles

    def window(ref):
        def of(u):
            start = pl.multiple_of((soft_first + u) * TILE, TILE)
            return ref[pl.ds(start, W + TILE), :]

        return of

    def outside(u, j):
        early = (soft_first + u + j) * TILE < W
        return jnp.where(jnp.logical_and(rank == 0, early), -1e30, 0.0)

    soft = soft_stages(
        rows, soft_q_ref, soft_ref, window(keys_ext), window(values_ext), before, after, outside
    )

    key_features = dot_nn(k_ref[...], map_ref[...]).astype(BF)
    tok = lax.broadcasted_iota(jnp.int32, (TILE, TILE), 0)
    carried = state[...]
    starts, features, inner = [], {}, {}
    for t in range(tiles):
        tl = slice(t * TILE, (t + 1) * TILE)
        starts.append(carried.astype(BF))
        carried = carried + dot_tn(key_features[tl, :], v_ref[tl, :])
    state[...] = carried

    def widen(t):
        sl = slice(t * rows, (t + 1) * rows)
        qs[sl, :] = q_ref[sl, :].astype(F32)

    def feature(t):
        features[t] = jnp.concatenate(
            [
                dot_nn(qs[pl.ds(t * rows + h, TILE, stride=heads), :].astype(BF), qmap_ref[h]).astype(BF)
                for h in range(heads)
            ],
            0,
        )

    def score(t):
        inner[t] = dot_nt(features[t], key_features[t * TILE : (t + 1) * TILE, :]).astype(BF) * keep[...]

    def combine(t):
        out = dot_nn(
            jnp.concatenate([inner.pop(t), features.pop(t)], 1),
            jnp.concatenate([v_ref[t * TILE : (t + 1) * TILE, :], starts[t]], 0),
        )
        factor = lax.rsqrt((tok + (first + t * TILE + 1)).astype(F32))
        for h in range(heads):
            os[pl.ds(t * rows + h, TILE, stride=heads), :] = out[h * TILE : (h + 1) * TILE, :] * factor

    def narrow(t):
        sl = slice(t * rows, (t + 1) * rows)
        o_ref[sl, :] = os[sl, :].astype(BF)

    apart = max(1, tiles // soft_tiles)

    def softmax_of(depth):
        def stage(t):
            if t % apart == 0 and t // apart < soft_tiles:
                soft[depth](t // apart)

        return stage

    def nothing(t):
        pass

    staged(
        tiles,
        lambda t: (softmax_of(0)(t), widen(t)),
        feature,
        lambda t: (softmax_of(1)(t), score(t)),
        combine,
        lambda t: (softmax_of(2)(t), narrow(t)),
    )


def per_device(ranks, queries, keys, values, query_maps, key_map, linear_cotangent):
    tokens, heads, head_dim = queries.shape
    chunk = CHUNK if tokens % CHUNK == 0 else W
    steps = tokens // chunk
    chunk_rows = chunk * heads
    tile_rows = TILE * heads
    slab = head_dim // ranks * heads
    params = pltpu.CompilerParams(vmem_limit_bytes=VMEM_LIMIT)
    q_rows = queries.reshape(tokens * heads, head_dim)
    c_rows = linear_cotangent.reshape(tokens * heads, head_dim)
    row_spec = pl.BlockSpec((chunk_rows, head_dim), lambda i: (i, 0))
    key_spec = pl.BlockSpec((chunk, head_dim), lambda i: (i, 0))

    def whole(shape):
        return pl.BlockSpec(shape, lambda i: (0,) * len(shape))

    packet = (ranks, head_dim + 2 * padded16(slab), head_dim)
    send, rim = pl.pallas_call(
        functools.partial(backward_kernel, heads, ranks, slab),
        grid=(steps,),
        in_specs=[row_spec, row_spec, key_spec, key_spec, whole(key_map.shape)],
        out_specs=[whole(packet), whole((2 * W, head_dim))],
        out_shape=[
            jax.ShapeDtypeStruct(packet, BF),
            jax.ShapeDtypeStruct((2 * W, head_dim), BF),
        ],
        scratch_shapes=[
            pltpu.VMEM((heads, head_dim, 2 * head_dim), F32),
            pltpu.VMEM((head_dim, head_dim), F32),
            pltpu.VMEM((tile_rows, TILE), BF),
            pltpu.VMEM((chunk_rows, head_dim), F32),
            pltpu.VMEM((chunk_rows, head_dim), F32),
            pltpu.VMEM((heads * head_dim, head_dim), F32),
            pltpu.VMEM((heads * head_dim, head_dim), F32),
        ],
        compiler_params=params,
        name="backward",
    )(q_rows, c_rows, keys, values, key_map)

    rim = lax.ppermute(rim, "seq", [(r, (r + 1) % ranks) for r in range(ranks)])
    got = lax.all_to_all(send, "seq", 0, 0)

    left_keys = pl.BlockSpec((W, head_dim), lambda i: (jnp.maximum(i * (chunk // W) - 1, 0), 0))
    bias = pltpu.VMEM((tile_rows, TILE), F32)
    soft_rows = pl.pallas_call(
        functools.partial(softmax_kernel, heads),
        grid=(steps,),
        in_specs=[row_spec, left_keys, key_spec, left_keys, key_spec],
        out_specs=row_spec,
        out_shape=jax.ShapeDtypeStruct(q_rows.shape, BF),
        scratch_shapes=[bias, bias],
        compiler_params=params,
        name="softmax",
    )(q_rows, keys, keys, values, values)

    soft_steps = max(n for n in (1, 2, 4) if n <= steps)
    soft_spec = pl.BlockSpec(
        (W // soft_steps * heads, head_dim), lambda i: (jnp.minimum(i, soft_steps - 1), 0)
    )
    in_vmem = pl.BlockSpec(memory_space=pltpu.VMEM)
    linear_rows, soft_rows, gradient = pl.pallas_call(
        functools.partial(forward_kernel, heads, ranks, slab, soft_steps),
        grid=(steps,),
        in_specs=[
            row_spec,
            key_spec,
            key_spec,
            whole(key_map.shape),
            whole(query_maps.shape),
            soft_spec,
            in_vmem,
            in_vmem,
            pl.BlockSpec(memory_space=pl.ANY),
        ],
        out_specs=[row_spec, soft_spec, whole((slab, head_dim))],
        out_shape=[
            jax.ShapeDtypeStruct(q_rows.shape, BF),
            jax.ShapeDtypeStruct(q_rows.shape, BF),
            jax.ShapeDtypeStruct((slab, head_dim), F32),
        ],
        scratch_shapes=[
            pltpu.VMEM((head_dim, head_dim), F32),
            pltpu.VMEM((tile_rows, TILE), BF),
            pltpu.VMEM((chunk_rows, head_dim), F32),
            pltpu.VMEM((chunk_rows, head_dim), F32),
            pltpu.VMEM((2 * W, head_dim), BF),
            pltpu.VMEM((2 * W, head_dim), BF),
            bias,
            bias,
        ],
        input_output_aliases={8: 1},
        compiler_params=params,
        name="forward",
    )(q_rows, keys, values, key_map, query_maps, q_rows, got, rim, soft_rows)

    return (
        soft_rows.reshape(queries.shape),
        linear_rows.reshape(queries.shape),
        gradient.reshape(head_dim // ranks, heads, head_dim),
    )


def solution(mesh):
    return jax.shard_map(
        functools.partial(per_device, mesh.shape["seq"]),
        mesh=mesh,
        in_specs=(
            P(("groups", "seq"), ("head", "rep"), None),
            P(("groups", "seq"), None),
            P(("groups", "seq"), None),
            P(("groups", "head", "rep"), None, None),
            P("groups", None),
            P(("groups", "seq"), ("head", "rep"), None),
        ),
        out_specs=(
            P(("groups", "seq"), ("head", "rep"), None),
            P(("groups", "seq"), ("head", "rep"), None),
            P(("groups", "seq"), ("head", "rep"), None),
        ),
        check_vma=False,
    )
```

```python
import functools

import jax
import jax.numpy as jnp
import numpy as np
from jax import lax
from jax.experimental import pallas as pl
from jax.experimental.pallas import tpu as pltpu
from jax.sharding import PartitionSpec as P

W = 512
TILE = 128
CHUNKS = (1024, 1024, 1024)
GROUP = 4
BF = jnp.bfloat16
F32 = jnp.float32
LOG2E = 1.4426950408889634
VMEM_LIMIT = 64 * 2**20 - 2**17


def dot_nn(a, b):
    return jnp.dot(a, b, preferred_element_type=F32)


def dot_nt(a, b):
    return lax.dot_general(a, b, (((1,), (1,)), ((), ())), preferred_element_type=F32)


def dot_tn(a, b):
    return lax.dot_general(a, b, (((0,), (0,)), ((), ())), preferred_element_type=F32)


def tokens_of_rows(rows, heads):
    return lax.broadcasted_iota(jnp.int32, (rows, TILE), 0) // heads


def padded16(rows):
    return -(-rows // 16) * 16


def staged(count, *stages):
    for x in range(count + len(stages) - 1):
        for depth in reversed(range(len(stages))):
            if 0 <= x - depth < count:
                stages[depth](x - depth)


def causal_keep(heads):
    tok = lax.broadcasted_iota(jnp.int32, (TILE, TILE), 0)
    causal = lax.broadcasted_iota(jnp.int32, (TILE, TILE), 1) <= tok
    return jnp.concatenate([jnp.where(causal, 1.0, 0.0)] * heads, 0).astype(BF)


def backward_kernel(
    heads, ranks, slab, q_ref, c_ref, k_ref, v_ref, map_ref, *refs
):
    send_refs, (acc, state, keep, qs, cs, gi, qi) = refs[:ranks], refs[ranks:]
    step, steps = pl.program_id(0), pl.num_programs(0)
    head_dim = map_ref.shape[0]
    tiles = k_ref.shape[0] // TILE
    rows = TILE * heads
    group = min(GROUP, tiles)

    @pl.when(step == 0)
    def _():
        acc[...] = jnp.zeros_like(acc)
        state[...] = jnp.zeros_like(state)
        keep[...] = causal_keep(heads)

    first = lax.axis_index("seq") * (steps * tiles * TILE) + step * (tiles * TILE)
    key_features = dot_nn(k_ref[...], map_ref[...]).astype(BF)
    carried = state[...]
    starts, cots, back, grads = [], {}, {}, {}
    for t in range(tiles):
        tl = slice(t * TILE, (t + 1) * TILE)
        starts.append(carried.astype(BF))
        carried = carried + dot_tn(v_ref[tl, :], key_features[tl, :])
    state[...] = carried

    def widen(t):
        sl = slice(t * rows, (t + 1) * rows)
        qs[sl, :] = q_ref[sl, :].astype(F32)
        cs[sl, :] = c_ref[sl, :].astype(F32)

    def part(ref, t, h, count=TILE):
        return ref[pl.ds(t * rows + h, count, stride=heads), :]

    def score(t):
        cots[t] = jnp.concatenate([part(cs, t, h).astype(BF) for h in range(heads)], 0)
        back[t] = dot_nt(cots[t], v_ref[t * TILE : (t + 1) * TILE, :]).astype(BF) * keep[...]

    def gradient(t):
        out = dot_nn(
            jnp.concatenate([back.pop(t), cots[t]], 1),
            jnp.concatenate([key_features[t * TILE : (t + 1) * TILE, :], starts[t]], 0),
        )
        grads[t] = out.astype(BF)

    def gather(t):
        if (t + 1) % group:
            return
        begin = t + 1 - group
        tok = lax.broadcasted_iota(jnp.int32, (group * TILE, head_dim), 0)
        factor = lax.rsqrt((tok + (first + begin * TILE + 1)).astype(F32))
        for h in range(heads):
            hs = slice(h * TILE, (h + 1) * TILE)
            right = jnp.concatenate(
                [
                    jnp.concatenate([grads[u][hs, :], cots[u][hs, :]], 1)
                    for u in range(begin, t + 1)
                ],
                0,
            )
            acc[h] += dot_tn((part(qs, begin, h, group * TILE) * factor).astype(BF), right)

    staged(tiles, widen, score, gradient, gather)

    @pl.when(step == steps - 1)
    def _():
        for h in range(heads):
            pick = pl.ds(h, head_dim, stride=heads)
            gi[pick, :] = acc[h, :, :head_dim]
            qi[pick, :] = acc[h, :, head_dim:]
        size = padded16(slab)
        for k, send_ref in enumerate(send_refs):
            begin = pl.multiple_of(lax.rem(lax.axis_index("seq") + k, ranks) * slab, slab)
            send_ref[:head_dim, :] = state[...].astype(BF)
            for n, terms in enumerate((gi, qi)):
                part = terms[pl.ds(begin, slab), :]
                if size > slab:
                    part = jnp.concatenate([part, jnp.zeros((size - slab, head_dim), F32)], 0)
                send_ref[head_dim + n * size : head_dim + (n + 1) * size, :] = part.astype(BF)
        if ranks > 1:
            send_refs[1][head_dim + 2 * size : head_dim + 2 * size + W, :] = k_ref[...][-W:, :]
            send_refs[1][head_dim + 2 * size + W :, :] = v_ref[...][-W:, :]


def window_biases(heads, before, after):
    rows = TILE * heads
    low = lax.broadcasted_iota(jnp.int32, (rows, TILE), 1) <= tokens_of_rows(rows, heads)
    before[...] = jnp.where(low, -1e30, 0.0)
    after[...] = jnp.where(low, 0.0, -1e30)


def soft_stages(rows, q_ref, o_ref, keys_of, values_of, before, after, extra):
    head_dim = q_ref.shape[1]
    scale = float(LOG2E / np.sqrt(head_dim))
    held, total = {}, {}

    def score(t):
        held[t] = dot_nt(q_ref[t * rows : (t + 1) * rows, :], keys_of(t))

    def weigh(t):
        scores = held[t]
        parts = [scores[:, j * TILE : (j + 1) * TILE] for j in range(W // TILE + 1)]
        parts[0] = parts[0] + before[...]
        parts[-1] = parts[-1] + after[...]
        if extra is not None:
            parts = [part if j == W // TILE else part + extra(t, j) for j, part in enumerate(parts)]
        highest = jnp.max(functools.reduce(jnp.maximum, parts), axis=1, keepdims=True)
        weights = [jnp.exp2((part - highest) * scale) for part in parts]
        total[t] = jnp.sum(functools.reduce(jnp.add, weights), axis=1, keepdims=True)
        held[t] = jnp.concatenate([weight.astype(BF) for weight in weights], 1)

    def combine(t):
        out = dot_nn(held.pop(t), values_of(t))
        o_ref[t * rows : (t + 1) * rows, :] = (out / total.pop(t)).astype(BF)

    return score, weigh, combine


def softmax_kernel(heads, q_ref, kb_ref, kh_ref, vb_ref, vh_ref, o_ref, before, after):
    @pl.when(pl.program_id(0) == 0)
    def _():
        window_biases(heads, before, after)

    def window(left, here):
        def of(t):
            start, end = t * TILE, (t + 1) * TILE
            if start >= W:
                return here[start - W : end, :]
            return jnp.concatenate([left[start:, :], here[:end, :]], 0)

        return of

    stages = soft_stages(
        TILE * heads, q_ref, o_ref, window(kb_ref, kh_ref), window(vb_ref, vh_ref), before, after, None
    )
    count = kh_ref.shape[0] // TILE
    skipped = W // TILE

    @pl.when(pl.program_id(0) == 0)
    def _():
        if count > skipped:
            staged(count - skipped, *(lambda t, stage=stage: stage(t + skipped) for stage in stages))

    @pl.when(pl.program_id(0) > 0)
    def _():
        staged(count, *stages)


def forward_kernel(
    heads, ranks, slab, soft_steps, q_ref, k_ref, v_ref, map_ref, qmap_ref, soft_q_ref, *refs
):
    got_refs, refs = refs[:ranks], refs[ranks + 1 :]
    o_ref, soft_ref, grad_ref, state, keep, qs, os, got, keys_ext, values_ext, before, after = refs
    step, steps = pl.program_id(0), pl.num_programs(0)
    head_dim = map_ref.shape[0]
    tokens = k_ref.shape[0]
    tiles = tokens // TILE
    rows = TILE * heads
    rank = lax.axis_index("seq")

    @pl.when(step == 0)
    def _():
        size = padded16(slab)
        length = head_dim + 2 * size
        for k, got_ref in enumerate(got_refs):
            got[lax.rem(rank - k + ranks, ranks)] = got_ref[:length, :]
        keys_ext[:W, :] = got_refs[1][length : length + W, :]
        values_ext[:W, :] = got_refs[1][length + W :, :]
        keys_ext[W:, :] = k_ref[:W, :]
        values_ext[W:, :] = v_ref[:W, :]
        window_biases(heads, before, after)
        keep[...] = causal_keep(heads)
        earlier = jnp.zeros((head_dim, head_dim), F32)
        mine = earlier
        grad = jnp.zeros((slab, head_dim), F32)
        for r in range(ranks):
            mine = jnp.where(rank == r, earlier, mine)
            middle = head_dim + size
            grad = grad + got[r, head_dim:middle, :].astype(F32)[:slab]
            if r:
                high = earlier.astype(BF)
                low = (earlier - high.astype(F32)).astype(BF)
                products = got[r, middle:, :]
                grad = grad + (dot_nn(products, high) + dot_nn(products, low))[:slab]
            earlier = earlier + got[r, :head_dim, :].astype(F32)
        grad_ref[...] = grad
        state[...] = mine.T

    first = rank * (steps * tokens) + step * tokens
    soft_tiles = soft_q_ref.shape[0] // rows
    soft_first = jnp.minimum(step, soft_steps - 1) * soft_tiles

    def window(ref):
        def of(u):
            start = pl.multiple_of((soft_first + u) * TILE, TILE)
            return ref[pl.ds(start, W + TILE), :]

        return of

    def outside(u, j):
        early = (soft_first + u + j) * TILE < W
        return jnp.where(jnp.logical_and(rank == 0, early), -1e30, 0.0)

    soft = soft_stages(
        rows, soft_q_ref, soft_ref, window(keys_ext), window(values_ext), before, after, outside
    )

    key_features = dot_nn(k_ref[...], map_ref[...]).astype(BF)
    tok = lax.broadcasted_iota(jnp.int32, (TILE, TILE), 0)
    carried = state[...]
    starts, features, inner = [], {}, {}
    for t in range(tiles):
        tl = slice(t * TILE, (t + 1) * TILE)
        starts.append(carried.astype(BF))
        carried = carried + dot_tn(key_features[tl, :], v_ref[tl, :])
    state[...] = carried

    def widen(t):
        sl = slice(t * rows, (t + 1) * rows)
        qs[sl, :] = q_ref[sl, :].astype(F32)

    def feature(t):
        if t % group:
            return
        count = min(group, tiles - t)
        wide = [
            dot_nn(
                qs[pl.ds(t * rows + h, count * TILE, stride=heads), :].astype(BF), qmap_ref[h]
            ).astype(BF)
            for h in range(heads)
        ]
        for u in range(count):
            features[t + u] = jnp.concatenate([x[u * TILE : (u + 1) * TILE, :] for x in wide], 0)

    def score(t):
        inner[t] = dot_nt(features[t], key_features[t * TILE : (t + 1) * TILE, :]).astype(BF) * keep[...]

    def combine(t):
        out = dot_nn(
            jnp.concatenate([inner.pop(t), features.pop(t)], 1),
            jnp.concatenate([v_ref[t * TILE : (t + 1) * TILE, :], starts[t]], 0),
        )
        factor = lax.rsqrt((tok + (first + t * TILE + 1)).astype(F32))
        for h in range(heads):
            os[pl.ds(t * rows + h, TILE, stride=heads), :] = out[h * TILE : (h + 1) * TILE, :] * factor

    def narrow(t):
        sl = slice(t * rows, (t + 1) * rows)
        o_ref[sl, :] = os[sl, :].astype(BF)

    apart = max(1, tiles // soft_tiles)
    group = min(GROUP, tiles)

    def softmax_of(depth):
        def stage(t):
            if t % apart == 0 and t // apart < soft_tiles:
                soft[depth](t // apart)

        return stage

    def nothing(t):
        pass

    staged(
        tiles,
        lambda t: (softmax_of(0)(t), widen(t)),
        *[lambda t: None] * (group - 1),
        feature,
        lambda t: (softmax_of(1)(t), score(t)),
        combine,
        lambda t: (softmax_of(2)(t), narrow(t)),
    )


def per_device(ranks, queries, keys, values, query_maps, key_map, linear_cotangent):
    tokens, heads, head_dim = queries.shape
    tile_rows = TILE * heads
    slab = head_dim // ranks * heads
    params = pltpu.CompilerParams(vmem_limit_bytes=VMEM_LIMIT)
    q_rows = queries.reshape(tokens * heads, head_dim)
    c_rows = linear_cotangent.reshape(tokens * heads, head_dim)

    def split(chunk):
        chunk = chunk if tokens % chunk == 0 else W
        rows = pl.BlockSpec((chunk * heads, head_dim), lambda i: (i, 0))
        return chunk, tokens // chunk, chunk * heads, rows, pl.BlockSpec((chunk, head_dim), lambda i: (i, 0))

    def whole(shape):
        return pl.BlockSpec(shape, lambda i: (0,) * len(shape))

    length = head_dim + 2 * padded16(slab)
    packets = [(length + 2 * W if k == 1 else length, head_dim) for k in range(ranks)]
    chunk, steps, chunk_rows, row_spec, key_spec = split(CHUNKS[0])
    send = pl.pallas_call(
        functools.partial(backward_kernel, heads, ranks, slab),
        grid=(steps,),
        in_specs=[row_spec, row_spec, key_spec, key_spec, whole(key_map.shape)],
        out_specs=[whole(packet) for packet in packets],
        out_shape=[jax.ShapeDtypeStruct(packet, BF) for packet in packets],
        scratch_shapes=[
            pltpu.VMEM((heads, head_dim, 2 * head_dim), F32),
            pltpu.VMEM((head_dim, head_dim), F32),
            pltpu.VMEM((tile_rows, TILE), BF),
            pltpu.VMEM((chunk_rows, head_dim), F32),
            pltpu.VMEM((chunk_rows, head_dim), F32),
            pltpu.VMEM((heads * head_dim, head_dim), F32),
            pltpu.VMEM((heads * head_dim, head_dim), F32),
        ],
        compiler_params=params,
        name="backward",
    )(q_rows, c_rows, keys, values, key_map)

    got = [
        lax.ppermute(part, "seq", [(r, (r + k) % ranks) for r in range(ranks)]) if k else part
        for k, part in enumerate(send)
    ]

    chunk, steps, chunk_rows, row_spec, key_spec = split(CHUNKS[1])
    left_keys = pl.BlockSpec((W, head_dim), lambda i, per=chunk // W: (jnp.maximum(i * per - 1, 0), 0))
    bias = pltpu.VMEM((tile_rows, TILE), F32)
    soft_rows = pl.pallas_call(
        functools.partial(softmax_kernel, heads),
        grid=(steps,),
        in_specs=[row_spec, left_keys, key_spec, left_keys, key_spec],
        out_specs=row_spec,
        out_shape=jax.ShapeDtypeStruct(q_rows.shape, BF),
        scratch_shapes=[bias, bias],
        compiler_params=params,
        name="softmax",
    )(q_rows, keys, keys, values, values)

    chunk, steps, chunk_rows, row_spec, key_spec = split(CHUNKS[2])
    soft_steps = max(n for n in (1, 2, 4) if n <= steps)
    soft_spec = pl.BlockSpec(
        (W // soft_steps * heads, head_dim), lambda i: (jnp.minimum(i, soft_steps - 1), 0)
    )
    in_vmem = pl.BlockSpec(memory_space=pltpu.VMEM)
    linear_rows, soft_rows, gradient = pl.pallas_call(
        functools.partial(forward_kernel, heads, ranks, slab, soft_steps),
        grid=(steps,),
        in_specs=[
            row_spec,
            key_spec,
            key_spec,
            whole(key_map.shape),
            whole(query_maps.shape),
            soft_spec,
            *[in_vmem] * ranks,
            pl.BlockSpec(memory_space=pl.ANY),
        ],
        out_specs=[row_spec, soft_spec, whole((slab, head_dim))],
        out_shape=[
            jax.ShapeDtypeStruct(q_rows.shape, BF),
            jax.ShapeDtypeStruct(q_rows.shape, BF),
            jax.ShapeDtypeStruct((slab, head_dim), F32),
        ],
        scratch_shapes=[
            pltpu.VMEM((head_dim, head_dim), F32),
            pltpu.VMEM((tile_rows, TILE), BF),
            pltpu.VMEM((chunk_rows, head_dim), F32),
            pltpu.VMEM((chunk_rows, head_dim), F32),
            pltpu.VMEM((ranks, length, head_dim), BF),
            pltpu.VMEM((2 * W, head_dim), BF),
            pltpu.VMEM((2 * W, head_dim), BF),
            bias,
            bias,
        ],
        input_output_aliases={6 + ranks: 1},
        compiler_params=params,
        name="forward",
    )(q_rows, keys, values, key_map, query_maps, q_rows, *got, soft_rows)

    return (
        soft_rows.reshape(queries.shape),
        linear_rows.reshape(queries.shape),
        gradient.reshape(head_dim // ranks, heads, head_dim),
    )


def solution(mesh):
    return jax.shard_map(
        functools.partial(per_device, mesh.shape["seq"]),
        mesh=mesh,
        in_specs=(
            P(("groups", "seq"), ("head", "rep"), None),
            P(("groups", "seq"), None),
            P(("groups", "seq"), None),
            P(("groups", "head", "rep"), None, None),
            P("groups", None),
            P(("groups", "seq"), ("head", "rep"), None),
        ),
        out_specs=(
            P(("groups", "seq"), ("head", "rep"), None),
            P(("groups", "seq"), ("head", "rep"), None),
            P(("groups", "seq"), ("head", "rep"), None),
        ),
        check_vma=False,
    )
```

```python
import functools

import jax
import jax.numpy as jnp
import numpy as np
from jax import lax
from jax.experimental import pallas as pl
from jax.experimental.pallas import tpu as pltpu
from jax.sharding import PartitionSpec as P

W = 512
TILE = 128
CHUNKS = (1024, 1024, 1024)
GROUP = 4
BF = jnp.bfloat16
F32 = jnp.float32
LOG2E = 1.4426950408889634
VMEM_LIMIT = 64 * 2**20 - 2**17


def dot_nn(a, b):
    return jnp.dot(a, b, preferred_element_type=F32)


def dot_nt(a, b):
    return lax.dot_general(a, b, (((1,), (1,)), ((), ())), preferred_element_type=F32)


def dot_tn(a, b):
    return lax.dot_general(a, b, (((0,), (0,)), ((), ())), preferred_element_type=F32)


def tokens_of_rows(rows, heads):
    return lax.broadcasted_iota(jnp.int32, (rows, TILE), 0) // heads


def padded16(rows):
    return -(-rows // 16) * 16


def staged(count, *stages):
    for x in range(count + len(stages) - 1):
        for depth in reversed(range(len(stages))):
            if 0 <= x - depth < count:
                stages[depth](x - depth)


def causal_keep(heads):
    tok = lax.broadcasted_iota(jnp.int32, (TILE, TILE), 0)
    causal = lax.broadcasted_iota(jnp.int32, (TILE, TILE), 1) <= tok
    return jnp.concatenate([jnp.where(causal, 1.0, 0.0)] * heads, 0).astype(BF)


def backward_kernel(
    heads, ranks, slab, q_ref, c_ref, k_ref, v_ref, map_ref, *refs
):
    send_refs, (acc, state, keep, qs, cs, gi, qi) = refs[:ranks], refs[ranks:]
    step, steps = pl.program_id(0), pl.num_programs(0)
    head_dim = map_ref.shape[0]
    tiles = k_ref.shape[0] // TILE
    rows = TILE * heads
    group = tiles

    @pl.when(step == 0)
    def _():
        acc[...] = jnp.zeros_like(acc)
        state[...] = jnp.zeros_like(state)
        keep[...] = causal_keep(heads)

    first = lax.axis_index("seq") * (steps * tiles * TILE) + step * (tiles * TILE)
    key_features = dot_nn(k_ref[...], map_ref[...]).astype(BF)
    carried = state[...]
    starts, cots, back, grads = [], {}, {}, {}
    for t in range(tiles):
        tl = slice(t * TILE, (t + 1) * TILE)
        starts.append(carried.astype(BF))
        carried = carried + dot_tn(v_ref[tl, :], key_features[tl, :])
    state[...] = carried

    def widen(t):
        sl = slice(t * rows, (t + 1) * rows)
        qs[sl, :] = q_ref[sl, :].astype(F32)
        cs[sl, :] = c_ref[sl, :].astype(F32)

    def part(ref, t, h, count=TILE):
        return ref[pl.ds(t * rows + h, count, stride=heads), :]

    def score(t):
        cots[t] = jnp.concatenate([part(cs, t, h).astype(BF) for h in range(heads)], 0)
        back[t] = dot_nt(cots[t], v_ref[t * TILE : (t + 1) * TILE, :]).astype(BF) * keep[...]

    def gradient(t):
        out = dot_nn(
            jnp.concatenate([back.pop(t), cots[t]], 1),
            jnp.concatenate([key_features[t * TILE : (t + 1) * TILE, :], starts[t]], 0),
        )
        grads[t] = out.astype(BF)

    def gather(t):
        if (t + 1) % group:
            return
        begin = t + 1 - group
        tok = lax.broadcasted_iota(jnp.int32, (group * TILE, head_dim), 0)
        factor = lax.rsqrt((tok + (first + begin * TILE + 1)).astype(F32))
        for h in range(heads):
            hs = slice(h * TILE, (h + 1) * TILE)
            right = jnp.concatenate(
                [
                    jnp.concatenate([grads[u][hs, :], cots[u][hs, :]], 1)
                    for u in range(begin, t + 1)
                ],
                0,
            )
            acc[h] += dot_tn((part(qs, begin, h, group * TILE) * factor).astype(BF), right)

    staged(tiles, widen, score, gradient, gather)

    @pl.when(step == steps - 1)
    def _():
        for h in range(heads):
            pick = pl.ds(h, head_dim, stride=heads)
            gi[pick, :] = acc[h, :, :head_dim]
            qi[pick, :] = acc[h, :, head_dim:]
        size = padded16(slab)
        for k, send_ref in enumerate(send_refs):
            begin = pl.multiple_of(lax.rem(lax.axis_index("seq") + k, ranks) * slab, slab)
            send_ref[:head_dim, :] = state[...].astype(BF)
            for n, terms in enumerate((gi, qi)):
                part = terms[pl.ds(begin, slab), :]
                if size > slab:
                    part = jnp.concatenate([part, jnp.zeros((size - slab, head_dim), F32)], 0)
                send_ref[head_dim + n * size : head_dim + (n + 1) * size, :] = part.astype(BF)
        if ranks > 1:
            send_refs[1][head_dim + 2 * size : head_dim + 2 * size + W, :] = k_ref[...][-W:, :]
            send_refs[1][head_dim + 2 * size + W :, :] = v_ref[...][-W:, :]


def window_masks(heads, late, keep_first, keep_last):
    rows = TILE * heads
    causal = lax.broadcasted_iota(jnp.int32, (rows, TILE), 1) <= tokens_of_rows(rows, heads)
    late[...] = jnp.where(causal, 1.0, 0.0)
    keep_last[...] = late[...].astype(BF)
    keep_first[...] = (1.0 - late[...]).astype(BF)


def soft_stages(rows, q_ref, o_ref, keys_of, values_of, masks, extra):
    head_dim = q_ref.shape[1]
    late, keep_first, keep_last = masks
    scale = float(LOG2E / np.sqrt(head_dim))
    held, total = {}, {}

    def score(t):
        held[t] = dot_nt(q_ref[t * rows : (t + 1) * rows, :], keys_of(t))

    def weigh(t):
        scores = held[t]
        parts = [scores[:, j * TILE : (j + 1) * TILE] for j in range(W // TILE + 1)]
        if extra is not None:
            parts = [part if j == W // TILE else part + extra(t, j) for j, part in enumerate(parts)]
        parts = [jnp.where(late[...] > 0.5, parts[-1], parts[0]), *parts[1:-1]]
        highest = jnp.max(functools.reduce(jnp.maximum, parts), axis=1, keepdims=True)
        weights = [jnp.exp2((part - highest) * scale) for part in parts]
        total[t] = jnp.sum(functools.reduce(jnp.add, weights), axis=1, keepdims=True)
        ends, *middle = [weight.astype(BF) for weight in weights]
        held[t] = jnp.concatenate([ends * keep_first[...], *middle, ends * keep_last[...]], 1)

    def combine(t):
        out = dot_nn(held.pop(t), values_of(t))
        o_ref[t * rows : (t + 1) * rows, :] = (out / total.pop(t)).astype(BF)

    return score, weigh, combine


def softmax_kernel(heads, q_ref, k_ref, v_ref, o_ref, *masks):
    @pl.when(pl.program_id(0) == 0)
    def _():
        window_masks(heads, *masks)

    def window(ref):
        return lambda t: ref[t * TILE : (t + 1) * TILE + W, :]

    stages = soft_stages(
        TILE * heads, q_ref, o_ref, window(k_ref), window(v_ref), masks, None
    )
    staged((k_ref.shape[0] - W) // TILE, *stages)


def forward_kernel(
    heads, ranks, slab, soft_steps, q_ref, k_ref, v_ref, map_ref, qmap_ref, soft_q_ref, *refs
):
    got_refs, refs = refs[:ranks], refs[ranks + 1 :]
    o_ref, soft_ref, grad_ref, state, keep, qs, os, got, keys_ext, values_ext, *masks = refs
    step, steps = pl.program_id(0), pl.num_programs(0)
    head_dim = map_ref.shape[0]
    tokens = k_ref.shape[0]
    tiles = tokens // TILE
    rows = TILE * heads
    rank = lax.axis_index("seq")

    @pl.when(step == 0)
    def _():
        size = padded16(slab)
        length = head_dim + 2 * size
        for k, got_ref in enumerate(got_refs):
            got[lax.rem(rank - k + ranks, ranks)] = got_ref[:length, :]
        keys_ext[:W, :] = got_refs[1][length : length + W, :]
        values_ext[:W, :] = got_refs[1][length + W :, :]
        keys_ext[W:, :] = k_ref[:W, :]
        values_ext[W:, :] = v_ref[:W, :]
        window_masks(heads, *masks)
        keep[...] = causal_keep(heads)
        earlier = jnp.zeros((head_dim, head_dim), F32)
        mine = earlier
        grad = jnp.zeros((slab, head_dim), F32)
        for r in range(ranks):
            mine = jnp.where(rank == r, earlier, mine)
            middle = head_dim + size
            grad = grad + got[r, head_dim:middle, :].astype(F32)[:slab]
            if r:
                high = earlier.astype(BF)
                low = (earlier - high.astype(F32)).astype(BF)
                products = got[r, middle:, :]
                grad = grad + (dot_nn(products, high) + dot_nn(products, low))[:slab]
            earlier = earlier + got[r, :head_dim, :].astype(F32)
        grad_ref[...] = grad
        state[...] = mine.T

    first = rank * (steps * tokens) + step * tokens
    soft_tiles = soft_q_ref.shape[0] // rows
    soft_first = jnp.minimum(step, soft_steps - 1) * soft_tiles

    def window(ref):
        def of(u):
            start = pl.multiple_of((soft_first + u) * TILE, TILE)
            return ref[pl.ds(start, W + TILE), :]

        return of

    def outside(u, j):
        early = (soft_first + u + j) * TILE < W
        return jnp.where(jnp.logical_and(rank == 0, early), -1e30, 0.0)

    soft = soft_stages(
        rows, soft_q_ref, soft_ref, window(keys_ext), window(values_ext), masks, outside
    )

    key_features = dot_nn(k_ref[...], map_ref[...]).astype(BF)
    tok = lax.broadcasted_iota(jnp.int32, (TILE, TILE), 0)
    carried = state[...]
    starts, features, inner = [], {}, {}
    for t in range(tiles):
        tl = slice(t * TILE, (t + 1) * TILE)
        starts.append(carried.astype(BF))
        carried = carried + dot_tn(key_features[tl, :], v_ref[tl, :])
    state[...] = carried

    def widen(t):
        sl = slice(t * rows, (t + 1) * rows)
        qs[sl, :] = q_ref[sl, :].astype(F32)

    def feature(t):
        if t % group:
            return
        count = min(group, tiles - t)
        wide = [
            dot_nn(
                qs[pl.ds(t * rows + h, count * TILE, stride=heads), :].astype(BF), qmap_ref[h]
            ).astype(BF)
            for h in range(heads)
        ]
        for u in range(count):
            features[t + u] = jnp.concatenate([x[u * TILE : (u + 1) * TILE, :] for x in wide], 0)

    def score(t):
        inner[t] = dot_nt(features[t], key_features[t * TILE : (t + 1) * TILE, :]).astype(BF) * keep[...]

    def combine(t):
        out = dot_nn(
            jnp.concatenate([inner.pop(t), features.pop(t)], 1),
            jnp.concatenate([v_ref[t * TILE : (t + 1) * TILE, :], starts[t]], 0),
        )
        factor = lax.rsqrt((tok + (first + t * TILE + 1)).astype(F32))
        for h in range(heads):
            os[pl.ds(t * rows + h, TILE, stride=heads), :] = out[h * TILE : (h + 1) * TILE, :] * factor

    def narrow(t):
        sl = slice(t * rows, (t + 1) * rows)
        o_ref[sl, :] = os[sl, :].astype(BF)

    apart = max(1, tiles // soft_tiles)
    group = min(GROUP, tiles)

    def softmax_of(depth):
        def stage(t):
            if t % apart == 0 and t // apart < soft_tiles:
                soft[depth](t // apart)

        return stage

    def nothing(t):
        pass

    staged(
        tiles,
        lambda t: (softmax_of(0)(t), widen(t)),
        *[lambda t: None] * (group - 1),
        feature,
        lambda t: (softmax_of(1)(t), score(t)),
        combine,
        lambda t: (softmax_of(2)(t), narrow(t)),
    )


def per_device(ranks, queries, keys, values, query_maps, key_map, linear_cotangent):
    tokens, heads, head_dim = queries.shape
    tile_rows = TILE * heads
    slab = head_dim // ranks * heads
    params = pltpu.CompilerParams(vmem_limit_bytes=VMEM_LIMIT)
    q_rows = queries.reshape(tokens * heads, head_dim)
    c_rows = linear_cotangent.reshape(tokens * heads, head_dim)

    def split(chunk):
        chunk = chunk if tokens % chunk == 0 else W
        rows = pl.BlockSpec((chunk * heads, head_dim), lambda i: (i, 0))
        return chunk, tokens // chunk, chunk * heads, rows, pl.BlockSpec((chunk, head_dim), lambda i: (i, 0))

    def whole(shape):
        return pl.BlockSpec(shape, lambda i: (0,) * len(shape))

    length = head_dim + 2 * padded16(slab)
    packets = [(length + 2 * W if k == 1 else length, head_dim) for k in range(ranks)]
    chunk, steps, chunk_rows, row_spec, key_spec = split(CHUNKS[0])
    send = pl.pallas_call(
        functools.partial(backward_kernel, heads, ranks, slab),
        grid=(steps,),
        in_specs=[row_spec, row_spec, key_spec, key_spec, whole(key_map.shape)],
        out_specs=[whole(packet) for packet in packets],
        out_shape=[jax.ShapeDtypeStruct(packet, BF) for packet in packets],
        scratch_shapes=[
            pltpu.VMEM((heads, head_dim, 2 * head_dim), F32),
            pltpu.VMEM((head_dim, head_dim), F32),
            pltpu.VMEM((tile_rows, TILE), BF),
            pltpu.VMEM((chunk_rows, head_dim), F32),
            pltpu.VMEM((chunk_rows, head_dim), F32),
            pltpu.VMEM((heads * head_dim, head_dim), F32),
            pltpu.VMEM((heads * head_dim, head_dim), F32),
        ],
        compiler_params=params,
        name="backward",
    )(q_rows, c_rows, keys, values, key_map)

    got = [
        lax.ppermute(part, "seq", [(r, (r + k) % ranks) for r in range(ranks)]) if k else part
        for k, part in enumerate(send)
    ]

    tiles = (tokens - W) // TILE
    per_step = max(n for n in range(1, CHUNKS[1] // TILE + 1) if tiles % n == 0)
    chunk = per_step * TILE
    later_rows = pl.BlockSpec(
        (pl.Element(chunk * heads), pl.Element(head_dim)), lambda i: (pl.multiple_of((W + i * chunk) * heads, TILE), 0)
    )
    window_keys = pl.BlockSpec(
        (pl.Element(W + chunk), pl.Element(head_dim)), lambda i: (pl.multiple_of(i * chunk, TILE), 0)
    )
    masks = [pltpu.VMEM((tile_rows, TILE), kind) for kind in (F32, BF, BF)]
    soft_rows = pl.pallas_call(
        functools.partial(softmax_kernel, heads),
        grid=(tiles // per_step,),
        in_specs=[later_rows, window_keys, window_keys],
        out_specs=later_rows,
        out_shape=jax.ShapeDtypeStruct(q_rows.shape, BF),
        scratch_shapes=masks,
        compiler_params=params,
        name="softmax",
    )(q_rows, keys, values)

    chunk, steps, chunk_rows, row_spec, key_spec = split(CHUNKS[2])
    soft_steps = max(n for n in (1, 2, 4) if n <= steps)
    soft_spec = pl.BlockSpec(
        (W // soft_steps * heads, head_dim), lambda i: (jnp.minimum(i, soft_steps - 1), 0)
    )
    in_vmem = pl.BlockSpec(memory_space=pltpu.VMEM)
    linear_rows, soft_rows, gradient = pl.pallas_call(
        functools.partial(forward_kernel, heads, ranks, slab, soft_steps),
        grid=(steps,),
        in_specs=[
            row_spec,
            key_spec,
            key_spec,
            whole(key_map.shape),
            whole(query_maps.shape),
            soft_spec,
            *[whole(packet) for packet in packets],
            pl.BlockSpec(memory_space=pl.ANY),
        ],
        out_specs=[row_spec, soft_spec, whole((slab, head_dim))],
        out_shape=[
            jax.ShapeDtypeStruct(q_rows.shape, BF),
            jax.ShapeDtypeStruct(q_rows.shape, BF),
            jax.ShapeDtypeStruct((slab, head_dim), F32),
        ],
        scratch_shapes=[
            pltpu.VMEM((head_dim, head_dim), F32),
            pltpu.VMEM((tile_rows, TILE), BF),
            pltpu.VMEM((chunk_rows, head_dim), F32),
            pltpu.VMEM((chunk_rows, head_dim), F32),
            pltpu.VMEM((ranks, length, head_dim), BF),
            pltpu.VMEM((2 * W, head_dim), BF),
            pltpu.VMEM((2 * W, head_dim), BF),
            *masks,
        ],
        input_output_aliases={6 + ranks: 1},
        compiler_params=params,
        name="forward",
    )(q_rows, keys, values, key_map, query_maps, q_rows, *got, soft_rows)

    return (
        soft_rows.reshape(queries.shape),
        linear_rows.reshape(queries.shape),
        gradient.reshape(head_dim // ranks, heads, head_dim),
    )


def solution(mesh):
    return jax.shard_map(
        functools.partial(per_device, mesh.shape["seq"]),
        mesh=mesh,
        in_specs=(
            P(("groups", "seq"), ("head", "rep"), None),
            P(("groups", "seq"), None),
            P(("groups", "seq"), None),
            P(("groups", "head", "rep"), None, None),
            P("groups", None),
            P(("groups", "seq"), ("head", "rep"), None),
        ),
        out_specs=(
            P(("groups", "seq"), ("head", "rep"), None),
            P(("groups", "seq"), ("head", "rep"), None),
            P(("groups", "seq"), ("head", "rep"), None),
        ),
        check_vma=False,
    )
```

```python
import functools

import jax
import jax.numpy as jnp
import numpy as np
from jax import lax
from jax.experimental import pallas as pl
from jax.experimental.pallas import tpu as pltpu
from jax.sharding import PartitionSpec as P

W = 512
TILE = 128
CHUNKS = (1024, 1024)
GROUP = 4
CUTS = (0, 2, 6, 12, 20)
BF = jnp.bfloat16
F32 = jnp.float32
LOG2E = 1.4426950408889634
VMEM_LIMIT = 64 * 2**20 - 2**17


def dot_nn(a, b):
    return jnp.dot(a, b, preferred_element_type=F32)


def dot_nt(a, b):
    return lax.dot_general(a, b, (((1,), (1,)), ((), ())), preferred_element_type=F32)


def dot_tn(a, b):
    return lax.dot_general(a, b, (((0,), (0,)), ((), ())), preferred_element_type=F32)


def tokens_of_rows(rows, heads):
    return lax.broadcasted_iota(jnp.int32, (rows, TILE), 0) // heads


def padded16(rows):
    return -(-rows // 16) * 16


def breadth(count, *stages):
    for stage in stages:
        for t in range(count):
            stage(t)


def staged(count, *stages):
    for x in range(count + len(stages) - 1):
        for depth in reversed(range(len(stages))):
            if 0 <= x - depth < count:
                stages[depth](x - depth)


def causal_keep(heads):
    tok = lax.broadcasted_iota(jnp.int32, (TILE, TILE), 0)
    causal = lax.broadcasted_iota(jnp.int32, (TILE, TILE), 1) <= tok
    return jnp.concatenate([jnp.where(causal, 1.0, 0.0)] * heads, 0).astype(BF)


def backward_kernel(
    heads, ranks, slab, q_ref, c_ref, k_ref, v_ref, map_ref, *refs
):
    send_refs, (acc, state, keep, qs, cs, gi, qi) = refs[:ranks], refs[ranks:]
    step, steps = pl.program_id(0), pl.num_programs(0)
    head_dim = map_ref.shape[0]
    tiles = k_ref.shape[0] // TILE
    rows = TILE * heads
    group = tiles

    @pl.when(step == 0)
    def _():
        acc[...] = jnp.zeros_like(acc)
        state[...] = jnp.zeros_like(state)
        keep[...] = causal_keep(heads)

    first = lax.axis_index("seq") * (steps * tiles * TILE) + step * (tiles * TILE)
    key_features = dot_nn(k_ref[...], map_ref[...]).astype(BF)
    carried = state[...]
    starts, cots, back, grads = [], {}, {}, {}
    for t in range(tiles):
        tl = slice(t * TILE, (t + 1) * TILE)
        starts.append(carried.astype(BF))
        carried = carried + dot_tn(v_ref[tl, :], key_features[tl, :])
    state[...] = carried

    def widen(t):
        sl = slice(t * rows, (t + 1) * rows)
        qs[sl, :] = q_ref[sl, :].astype(F32)
        cs[sl, :] = c_ref[sl, :].astype(F32)

    def part(ref, t, h, count=TILE):
        return ref[pl.ds(t * rows + h, count, stride=heads), :]

    def score(t):
        cots[t] = jnp.concatenate([part(cs, t, h).astype(BF) for h in range(heads)], 0)
        back[t] = dot_nt(cots[t], v_ref[t * TILE : (t + 1) * TILE, :]).astype(BF) * keep[...]

    def gradient(t):
        out = dot_nn(
            jnp.concatenate([back.pop(t), cots[t]], 1),
            jnp.concatenate([key_features[t * TILE : (t + 1) * TILE, :], starts[t]], 0),
        )
        grads[t] = out.astype(BF)

    def gather(t):
        if (t + 1) % group:
            return
        begin = t + 1 - group
        tok = lax.broadcasted_iota(jnp.int32, (group * TILE, head_dim), 0)
        factor = lax.rsqrt((tok + (first + begin * TILE + 1)).astype(F32))
        for h in range(heads):
            hs = slice(h * TILE, (h + 1) * TILE)
            right = jnp.concatenate(
                [
                    jnp.concatenate([grads[u][hs, :], cots[u][hs, :]], 1)
                    for u in range(begin, t + 1)
                ],
                0,
            )
            acc[h] += dot_tn((part(qs, begin, h, group * TILE) * factor).astype(BF), right)

    breadth(tiles, widen, score, gradient, gather)

    @pl.when(step == steps - 1)
    def _():
        for h in range(heads):
            pick = pl.ds(h, head_dim, stride=heads)
            gi[pick, :] = acc[h, :, :head_dim]
            qi[pick, :] = acc[h, :, head_dim:]
        size = padded16(slab)
        for k, send_ref in enumerate(send_refs):
            begin = pl.multiple_of(lax.rem(lax.axis_index("seq") + k, ranks) * slab, slab)
            send_ref[:head_dim, :] = state[...].astype(BF)
            for n, terms in enumerate((gi, qi)):
                part = terms[pl.ds(begin, slab), :]
                if size > slab:
                    part = jnp.concatenate([part, jnp.zeros((size - slab, head_dim), F32)], 0)
                send_ref[head_dim + n * size : head_dim + (n + 1) * size, :] = part.astype(BF)
        if ranks > 1:
            send_refs[1][head_dim + 2 * size : head_dim + 2 * size + W, :] = k_ref[...][-W:, :]
            send_refs[1][head_dim + 2 * size + W :, :] = v_ref[...][-W:, :]


def window_masks(heads, late, keep_first, keep_last):
    rows = TILE * heads
    causal = lax.broadcasted_iota(jnp.int32, (rows, TILE), 1) <= tokens_of_rows(rows, heads)
    late[...] = jnp.where(causal, 1.0, 0.0)
    keep_last[...] = late[...].astype(BF)
    keep_first[...] = (1.0 - late[...]).astype(BF)


def soft_stages(rows, q_ref, o_ref, keys_of, values_of, masks, extra):
    head_dim = q_ref.shape[1]
    late, keep_first, keep_last = masks
    scale = float(LOG2E / np.sqrt(head_dim))
    held, total = {}, {}

    def score(t):
        held[t] = dot_nt(q_ref[t * rows : (t + 1) * rows, :], keys_of(t))

    def weigh(t):
        scores = held[t]
        parts = [scores[:, j * TILE : (j + 1) * TILE] for j in range(W // TILE + 1)]
        if extra is not None:
            parts = [part if j == W // TILE else part + extra(t, j) for j, part in enumerate(parts)]
        parts = [jnp.where(lax.broadcasted_iota(jnp.int32, (rows, TILE), 1) <= lax.broadcasted_iota(jnp.int32, (rows, TILE), 0) // (rows // TILE), parts[-1], parts[0]), *parts[1:-1]]
        highest = jnp.max(functools.reduce(jnp.maximum, parts), axis=1, keepdims=True)
        weights = [jnp.exp2((part - highest) * scale) for part in parts]
        total[t] = jnp.sum(functools.reduce(jnp.add, weights), axis=1, keepdims=True)
        ends, *middle = [weight.astype(BF) for weight in weights]
        held[t] = jnp.concatenate([ends * keep_first[...], *middle, ends * keep_last[...]], 1)

    def combine(t):
        out = dot_nn(held.pop(t), values_of(t))
        o_ref[t * rows : (t + 1) * rows, :] = (out / total.pop(t)).astype(BF)

    return score, weigh, combine


def softmax_kernel(
    heads, cuts, q_hbm, k_hbm, v_hbm, o_hbm, late, keep_first, keep_last, q_all, k_all, v_all, o_all, ins, outs
):
    rows = TILE * heads
    tiles = q_all.shape[0] // rows

    def piece(n):
        begin, end = cuts[n], cuts[n + 1] if n + 1 < len(cuts) else tiles
        left = begin * TILE + W if n else 0
        right = end * TILE + W
        return [
            pltpu.make_async_copy(
                q_hbm.at[W * heads + begin * rows : W * heads + end * rows],
                q_all.at[begin * rows : end * rows],
                ins.at[0, n],
            ),
            pltpu.make_async_copy(k_hbm.at[left:right], k_all.at[left:right], ins.at[1, n]),
            pltpu.make_async_copy(v_hbm.at[left:right], v_all.at[left:right], ins.at[2, n]),
        ]

    def result(t):
        return pltpu.make_async_copy(
            o_all.at[t * rows : (t + 1) * rows],
            o_hbm.at[W * heads + t * rows : W * heads + (t + 1) * rows],
            outs.at[t],
        )

    for n in range(len(cuts)):
        for copy in piece(n):
            copy.start()
    window_masks(heads, late, keep_first, keep_last)

    def window(ref):
        return lambda t: ref[t * TILE : (t + 1) * TILE + W, :]

    score, weigh, combine = soft_stages(
        rows, q_all, o_all, window(k_all), window(v_all), (late, keep_first, keep_last), None
    )

    def first(t):
        if t in cuts:
            for copy in piece(cuts.index(t)):
                copy.wait()
        score(t)

    def last(t):
        combine(t)
        result(t).start()

    staged(tiles, first, weigh, last)
    for t in range(tiles):
        result(t).wait()


def forward_kernel(
    heads, ranks, slab, soft_steps, q_ref, k_ref, v_ref, map_ref, qmap_ref, soft_q_ref, *refs
):
    got_refs, refs = refs[:ranks], refs[ranks + 1 :]
    o_ref, soft_ref, grad_ref, state, keep, qs, os, got, keys_ext, values_ext, *masks = refs
    step, steps = pl.program_id(0), pl.num_programs(0)
    head_dim = map_ref.shape[0]
    tokens = k_ref.shape[0]
    tiles = tokens // TILE
    rows = TILE * heads
    rank = lax.axis_index("seq")

    @pl.when(step == 0)
    def _():
        size = padded16(slab)
        length = head_dim + 2 * size
        for k, got_ref in enumerate(got_refs):
            got[lax.rem(rank - k + ranks, ranks)] = got_ref[:length, :]
        keys_ext[:W, :] = got_refs[1][length : length + W, :]
        values_ext[:W, :] = got_refs[1][length + W :, :]
        keys_ext[W:, :] = k_ref[:W, :]
        values_ext[W:, :] = v_ref[:W, :]
        window_masks(heads, *masks)
        keep[...] = causal_keep(heads)
        earlier = jnp.zeros((head_dim, head_dim), F32)
        mine = earlier
        grad = jnp.zeros((slab, head_dim), F32)
        for r in range(ranks):
            mine = jnp.where(rank == r, earlier, mine)
            middle = head_dim + size
            grad = grad + got[r, head_dim:middle, :].astype(F32)[:slab]
            if r:
                high = earlier.astype(BF)
                low = (earlier - high.astype(F32)).astype(BF)
                products = got[r, middle:, :]
                grad = grad + (dot_nn(products, high) + dot_nn(products, low))[:slab]
            earlier = earlier + got[r, :head_dim, :].astype(F32)
        grad_ref[...] = grad
        state[...] = mine.T

    first = rank * (steps * tokens) + step * tokens
    soft_tiles = soft_q_ref.shape[0] // rows
    soft_first = jnp.minimum(step, soft_steps - 1) * soft_tiles

    def window(ref):
        def of(u):
            start = pl.multiple_of((soft_first + u) * TILE, TILE)
            return ref[pl.ds(start, W + TILE), :]

        return of

    def outside(u, j):
        early = (soft_first + u + j) * TILE < W
        return jnp.where(jnp.logical_and(rank == 0, early), -1e30, 0.0)

    soft = soft_stages(
        rows, soft_q_ref, soft_ref, window(keys_ext), window(values_ext), masks, outside
    )

    key_features = dot_nn(k_ref[...], map_ref[...]).astype(BF)
    tok = lax.broadcasted_iota(jnp.int32, (TILE, TILE), 0)
    carried = state[...]
    starts, features, inner = [], {}, {}
    for t in range(tiles):
        tl = slice(t * TILE, (t + 1) * TILE)
        starts.append(carried.astype(BF))
        carried = carried + dot_tn(key_features[tl, :], v_ref[tl, :])
    state[...] = carried

    def widen(t):
        sl = slice(t * rows, (t + 1) * rows)
        qs[sl, :] = q_ref[sl, :].astype(F32)

    def feature(t):
        if t % group:
            return
        count = min(group, tiles - t)
        wide = [
            dot_nn(
                qs[pl.ds(t * rows + h, count * TILE, stride=heads), :].astype(BF), qmap_ref[h]
            ).astype(BF)
            for h in range(heads)
        ]
        for u in range(count):
            features[t + u] = jnp.concatenate([x[u * TILE : (u + 1) * TILE, :] for x in wide], 0)

    def score(t):
        inner[t] = dot_nt(features[t], key_features[t * TILE : (t + 1) * TILE, :]).astype(BF) * keep[...]

    def combine(t):
        out = dot_nn(
            jnp.concatenate([inner.pop(t), features.pop(t)], 1),
            jnp.concatenate([v_ref[t * TILE : (t + 1) * TILE, :], starts[t]], 0),
        )
        factor = lax.rsqrt((tok + (first + t * TILE + 1)).astype(F32))
        for h in range(heads):
            os[pl.ds(t * rows + h, TILE, stride=heads), :] = out[h * TILE : (h + 1) * TILE, :] * factor

    def narrow(t):
        sl = slice(t * rows, (t + 1) * rows)
        o_ref[sl, :] = os[sl, :].astype(BF)

    apart = max(1, tiles // soft_tiles)
    group = min(GROUP, tiles)

    def softmax_of(depth):
        def stage(t):
            if t % apart == 0 and t // apart < soft_tiles:
                soft[depth](t // apart)

        return stage

    def nothing(t):
        pass

    breadth(
        tiles,
        lambda t: (softmax_of(0)(t), widen(t)),
        *[lambda t: None] * (group - 1),
        feature,
        lambda t: (softmax_of(1)(t), score(t)),
        combine,
        lambda t: (softmax_of(2)(t), narrow(t)),
    )


def per_device(ranks, queries, keys, values, query_maps, key_map, linear_cotangent):
    tokens, heads, head_dim = queries.shape
    tile_rows = TILE * heads
    slab = head_dim // ranks * heads
    params = pltpu.CompilerParams(vmem_limit_bytes=VMEM_LIMIT)
    q_rows = queries.reshape(tokens * heads, head_dim)
    c_rows = linear_cotangent.reshape(tokens * heads, head_dim)

    def split(chunk):
        chunk = chunk if tokens % chunk == 0 else W
        rows = pl.BlockSpec((chunk * heads, head_dim), lambda i: (i, 0))
        return chunk, tokens // chunk, chunk * heads, rows, pl.BlockSpec((chunk, head_dim), lambda i: (i, 0))

    def whole(shape):
        return pl.BlockSpec(shape, lambda i: (0,) * len(shape))

    length = head_dim + 2 * padded16(slab)
    packets = [(length + 2 * W if k == 1 else length, head_dim) for k in range(ranks)]
    chunk, steps, chunk_rows, row_spec, key_spec = split(CHUNKS[0])
    send = pl.pallas_call(
        functools.partial(backward_kernel, heads, ranks, slab),
        grid=(steps,),
        in_specs=[row_spec, row_spec, key_spec, key_spec, whole(key_map.shape)],
        out_specs=[whole(packet) for packet in packets],
        out_shape=[jax.ShapeDtypeStruct(packet, BF) for packet in packets],
        scratch_shapes=[
            pltpu.VMEM((heads, head_dim, 2 * head_dim), F32),
            pltpu.VMEM((head_dim, head_dim), F32),
            pltpu.VMEM((tile_rows, TILE), BF),
            pltpu.VMEM((chunk_rows, head_dim), F32),
            pltpu.VMEM((chunk_rows, head_dim), F32),
            pltpu.VMEM((heads * head_dim, head_dim), F32),
            pltpu.VMEM((heads * head_dim, head_dim), F32),
        ],
        compiler_params=params,
        name="backward",
    )(q_rows, c_rows, keys, values, key_map)

    got = [
        lax.ppermute(part, "seq", [(r, (r + k) % ranks) for r in range(ranks)]) if k else part
        for k, part in enumerate(send)
    ]

    tiles = (tokens - W) // TILE
    cuts = [t for t in CUTS if t < tiles]
    masks = [pltpu.VMEM((tile_rows, TILE), kind) for kind in (F32, BF, BF)]
    in_hbm = pl.BlockSpec(memory_space=pl.ANY)
    soft_rows = pl.pallas_call(
        functools.partial(softmax_kernel, heads, cuts),
        in_specs=[in_hbm] * 3,
        out_specs=in_hbm,
        out_shape=jax.ShapeDtypeStruct(q_rows.shape, BF),
        scratch_shapes=[
            *masks,
            pltpu.VMEM((tiles * tile_rows, head_dim), BF),
            pltpu.VMEM(keys.shape, BF),
            pltpu.VMEM(keys.shape, BF),
            pltpu.VMEM((tiles * tile_rows, head_dim), BF),
            pltpu.SemaphoreType.DMA((3, len(cuts))),
            pltpu.SemaphoreType.DMA((tiles,)),
        ],
        compiler_params=params,
        name="softmax",
    )(q_rows, keys, values)

    chunk, steps, chunk_rows, row_spec, key_spec = split(CHUNKS[1])
    soft_steps = max(n for n in (1, 2, 4) if n <= steps)
    soft_spec = pl.BlockSpec(
        (W // soft_steps * heads, head_dim), lambda i: (jnp.minimum(i, soft_steps - 1), 0)
    )
    in_vmem = pl.BlockSpec(memory_space=pltpu.VMEM)
    linear_rows, soft_rows, gradient = pl.pallas_call(
        functools.partial(forward_kernel, heads, ranks, slab, soft_steps),
        grid=(steps,),
        in_specs=[
            row_spec,
            key_spec,
            key_spec,
            whole(key_map.shape),
            whole(query_maps.shape),
            soft_spec,
            *[whole(packet) for packet in packets],
            pl.BlockSpec(memory_space=pl.ANY),
        ],
        out_specs=[row_spec, soft_spec, whole((slab, head_dim))],
        out_shape=[
            jax.ShapeDtypeStruct(q_rows.shape, BF),
            jax.ShapeDtypeStruct(q_rows.shape, BF),
            jax.ShapeDtypeStruct((slab, head_dim), F32),
        ],
        scratch_shapes=[
            pltpu.VMEM((head_dim, head_dim), F32),
            pltpu.VMEM((tile_rows, TILE), BF),
            pltpu.VMEM((chunk_rows, head_dim), F32),
            pltpu.VMEM((chunk_rows, head_dim), F32),
            pltpu.VMEM((ranks, length, head_dim), BF),
            pltpu.VMEM((2 * W, head_dim), BF),
            pltpu.VMEM((2 * W, head_dim), BF),
            *masks,
        ],
        input_output_aliases={6 + ranks: 1},
        compiler_params=params,
        name="forward",
    )(q_rows, keys, values, key_map, query_maps, q_rows, *got, soft_rows)

    return (
        soft_rows.reshape(queries.shape),
        linear_rows.reshape(queries.shape),
        gradient.reshape(head_dim // ranks, heads, head_dim),
    )


def solution(mesh):
    return jax.shard_map(
        functools.partial(per_device, mesh.shape["seq"]),
        mesh=mesh,
        in_specs=(
            P(("groups", "seq"), ("head", "rep"), None),
            P(("groups", "seq"), None),
            P(("groups", "seq"), None),
            P(("groups", "head", "rep"), None, None),
            P("groups", None),
            P(("groups", "seq"), ("head", "rep"), None),
        ),
        out_specs=(
            P(("groups", "seq"), ("head", "rep"), None),
            P(("groups", "seq"), ("head", "rep"), None),
            P(("groups", "seq"), ("head", "rep"), None),
        ),
        check_vma=False,
    )
```

```python
import functools

import jax
import jax.numpy as jnp
import numpy as np
from jax import lax
from jax.experimental import pallas as pl
from jax.experimental.pallas import tpu as pltpu
from jax.sharding import PartitionSpec as P

W = 512
TILE = 128
CHUNKS = (1024, 1024)
GROUP = 4
CUTS = (0, 2, 6, 12, 20)
BF = jnp.bfloat16
F32 = jnp.float32
LOG2E = 1.4426950408889634
VMEM_LIMIT = 64 * 2**20 - 2**17


def dot_nn(a, b):
    return jnp.dot(a, b, preferred_element_type=F32)


def dot_nt(a, b):
    return lax.dot_general(a, b, (((1,), (1,)), ((), ())), preferred_element_type=F32)


def dot_tn(a, b):
    return lax.dot_general(a, b, (((0,), (0,)), ((), ())), preferred_element_type=F32)


def tokens_of_rows(rows, heads):
    return lax.broadcasted_iota(jnp.int32, (rows, TILE), 0) // heads


def padded16(rows):
    return -(-rows // 16) * 16


def breadth(count, *stages):
    for stage in stages:
        for t in range(count):
            stage(t)


def staged(count, *stages):
    for x in range(count + len(stages) - 1):
        for depth in reversed(range(len(stages))):
            if 0 <= x - depth < count:
                stages[depth](x - depth)


def causal_keep(heads):
    tok = lax.broadcasted_iota(jnp.int32, (TILE, TILE), 0)
    causal = lax.broadcasted_iota(jnp.int32, (TILE, TILE), 1) <= tok
    return jnp.concatenate([jnp.where(causal, 1.0, 0.0)] * heads, 0).astype(BF)


def backward_kernel(
    heads, ranks, slab, q_ref, c_ref, k_ref, v_ref, map_ref, *refs
):
    send_refs, (acc, state, keep, qs, cs, gi, qi) = refs[:ranks], refs[ranks:]
    step, steps = pl.program_id(0), pl.num_programs(0)
    head_dim = map_ref.shape[0]
    tiles = k_ref.shape[0] // TILE
    rows = TILE * heads
    group = tiles

    @pl.when(step == 0)
    def _():
        acc[...] = jnp.zeros_like(acc)
        state[...] = jnp.zeros_like(state)
        keep[...] = causal_keep(heads)

    first = lax.axis_index("seq") * (steps * tiles * TILE) + step * (tiles * TILE)
    key_features = dot_nn(k_ref[...], map_ref[...]).astype(BF)
    carried = state[...]
    starts, cots, back, grads = [], {}, {}, {}
    for t in range(tiles):
        tl = slice(t * TILE, (t + 1) * TILE)
        starts.append(carried.astype(BF))
        carried = carried + dot_tn(v_ref[tl, :], key_features[tl, :])
    state[...] = carried

    def widen(t):
        sl = slice(t * rows, (t + 1) * rows)
        qs[sl, :] = q_ref[sl, :].astype(F32)
        cs[sl, :] = c_ref[sl, :].astype(F32)

    def part(ref, t, h, count=TILE):
        return ref[pl.ds(t * rows + h, count, stride=heads), :]

    def score(t):
        cots[t] = jnp.concatenate([part(cs, t, h).astype(BF) for h in range(heads)], 0)
        back[t] = dot_nt(cots[t], v_ref[t * TILE : (t + 1) * TILE, :]).astype(BF) * keep[...]

    def gradient(t):
        out = dot_nn(
            jnp.concatenate([back.pop(t), cots[t]], 1),
            jnp.concatenate([key_features[t * TILE : (t + 1) * TILE, :], starts[t]], 0),
        )
        grads[t] = out.astype(BF)

    def gather(t):
        if (t + 1) % group:
            return
        begin = t + 1 - group
        tok = lax.broadcasted_iota(jnp.int32, (group * TILE, head_dim), 0)
        factor = lax.rsqrt((tok + (first + begin * TILE + 1)).astype(F32))
        for h in range(heads):
            hs = slice(h * TILE, (h + 1) * TILE)
            right = jnp.concatenate(
                [
                    jnp.concatenate([grads[u][hs, :], cots[u][hs, :]], 1)
                    for u in range(begin, t + 1)
                ],
                0,
            )
            acc[h] += dot_tn((part(qs, begin, h, group * TILE) * factor).astype(BF), right)

    breadth(tiles, widen, score, gradient, gather)

    @pl.when(step == steps - 1)
    def _():
        for h in range(heads):
            pick = pl.ds(h, head_dim, stride=heads)
            gi[pick, :] = acc[h, :, :head_dim]
            qi[pick, :] = acc[h, :, head_dim:]
        size = padded16(slab)
        for k, send_ref in enumerate(send_refs):
            begin = pl.multiple_of(lax.rem(lax.axis_index("seq") + k, ranks) * slab, slab)
            send_ref[:head_dim, :] = state[...].astype(BF)
            for n, terms in enumerate((gi, qi)):
                part = terms[pl.ds(begin, slab), :]
                if size > slab:
                    part = jnp.concatenate([part, jnp.zeros((size - slab, head_dim), F32)], 0)
                send_ref[head_dim + n * size : head_dim + (n + 1) * size, :] = part.astype(BF)
        if ranks > 1:
            send_refs[1][head_dim + 2 * size : head_dim + 2 * size + W, :] = k_ref[...][-W:, :]
            send_refs[1][head_dim + 2 * size + W :, :] = v_ref[...][-W:, :]


def window_masks(heads, late, keep_first, keep_last):
    rows = TILE * heads
    causal = lax.broadcasted_iota(jnp.int32, (rows, TILE), 1) <= tokens_of_rows(rows, heads)
    late[...] = jnp.where(causal, 1.0, 0.0)
    keep_last[...] = late[...].astype(BF)
    keep_first[...] = (1.0 - late[...]).astype(BF)


def soft_stages(rows, q_ref, o_ref, keys_of, values_of, masks, extra):
    head_dim = q_ref.shape[1]
    late, keep_first, keep_last = masks
    scale = float(LOG2E / np.sqrt(head_dim))
    held, total = {}, {}

    def score(t):
        held[t] = dot_nt(q_ref[t * rows : (t + 1) * rows, :], keys_of(t))

    def weigh(t):
        scores = held[t]
        parts = [scores[:, j * TILE : (j + 1) * TILE] for j in range(W // TILE + 1)]
        if extra is not None:
            parts = [part if j == W // TILE else part + extra(t, j) for j, part in enumerate(parts)]
        parts = [jnp.where(lax.broadcasted_iota(jnp.int32, (rows, TILE), 1) <= lax.broadcasted_iota(jnp.int32, (rows, TILE), 0) // (rows // TILE), parts[-1], parts[0]), *parts[1:-1]]
        highest = jnp.max(functools.reduce(jnp.maximum, parts), axis=1, keepdims=True)
        weights = [jnp.exp2((part - highest) * scale) for part in parts]
        total[t] = jnp.sum(functools.reduce(jnp.add, weights), axis=1, keepdims=True)
        ends, *middle = [weight.astype(BF) for weight in weights]
        held[t] = jnp.concatenate([ends * keep_first[...], *middle, ends * keep_last[...]], 1)

    def combine(t):
        out = dot_nn(held.pop(t), values_of(t))
        o_ref[t * rows : (t + 1) * rows, :] = (out / total.pop(t)).astype(BF)

    return score, weigh, combine


def softmax_kernel(
    heads, cuts, q_hbm, k_hbm, v_hbm, o_hbm, late, keep_first, keep_last, q_all, k_all, v_all, o_all, ins, outs
):
    rows = TILE * heads
    tiles = q_all.shape[0] // rows

    def piece(n):
        begin, end = cuts[n], cuts[n + 1] if n + 1 < len(cuts) else tiles
        left = begin * TILE + W if n else 0
        right = end * TILE + W
        return [
            pltpu.make_async_copy(
                q_hbm.at[W * heads + begin * rows : W * heads + end * rows],
                q_all.at[begin * rows : end * rows],
                ins.at[0, n],
            ),
            pltpu.make_async_copy(k_hbm.at[left:right], k_all.at[left:right], ins.at[1, n]),
            pltpu.make_async_copy(v_hbm.at[left:right], v_all.at[left:right], ins.at[2, n]),
        ]

    def result(t):
        return pltpu.make_async_copy(
            o_all.at[t * rows : (t + 1) * rows],
            o_hbm.at[W * heads + t * rows : W * heads + (t + 1) * rows],
            outs.at[t],
        )

    for n in range(min(2, len(cuts))):
        for copy in piece(n):
            copy.start()
    window_masks(heads, late, keep_first, keep_last)

    def window(ref):
        return lambda t: ref[t * TILE : (t + 1) * TILE + W, :]

    score, weigh, combine = soft_stages(
        rows, q_all, o_all, window(k_all), window(v_all), (late, keep_first, keep_last), None
    )

    def first(t):
        if t in cuts:
            n = cuts.index(t)
            for copy in piece(n):
                copy.wait()
            if n + 2 < len(cuts):
                for copy in piece(n + 2):
                    copy.start()
        score(t)

    def last(t):
        combine(t)
        result(t).start()

    staged(tiles, first, weigh, last)
    for t in range(tiles):
        result(t).wait()


def forward_kernel(
    heads, ranks, slab, soft_steps, q_ref, k_ref, v_ref, map_ref, qmap_ref, soft_q_ref, *refs
):
    got_refs, refs = refs[:ranks], refs[ranks + 1 :]
    o_ref, soft_ref, grad_ref, state, keep, qs, os, got, keys_ext, values_ext, *masks = refs
    step, steps = pl.program_id(0), pl.num_programs(0)
    head_dim = map_ref.shape[0]
    tokens = k_ref.shape[0]
    tiles = tokens // TILE
    rows = TILE * heads
    rank = lax.axis_index("seq")

    @pl.when(step == 0)
    def _():
        size = padded16(slab)
        length = head_dim + 2 * size
        for k, got_ref in enumerate(got_refs):
            got[lax.rem(rank - k + ranks, ranks)] = got_ref[:length, :]
        keys_ext[:W, :] = got_refs[1][length : length + W, :]
        values_ext[:W, :] = got_refs[1][length + W :, :]
        keys_ext[W:, :] = k_ref[:W, :]
        values_ext[W:, :] = v_ref[:W, :]
        window_masks(heads, *masks)
        keep[...] = causal_keep(heads)
        earlier = jnp.zeros((head_dim, head_dim), F32)
        mine = earlier
        grad = jnp.zeros((slab, head_dim), F32)
        for r in range(ranks):
            mine = jnp.where(rank == r, earlier, mine)
            middle = head_dim + size
            grad = grad + got[r, head_dim:middle, :].astype(F32)[:slab]
            if r:
                high = earlier.astype(BF)
                low = (earlier - high.astype(F32)).astype(BF)
                products = got[r, middle:, :]
                grad = grad + (dot_nn(products, high) + dot_nn(products, low))[:slab]
            earlier = earlier + got[r, :head_dim, :].astype(F32)
        grad_ref[...] = grad
        state[...] = mine.T

    first = rank * (steps * tokens) + step * tokens
    soft_tiles = soft_q_ref.shape[0] // rows
    soft_first = jnp.minimum(step, soft_steps - 1) * soft_tiles

    def window(ref):
        def of(u):
            start = pl.multiple_of((soft_first + u) * TILE, TILE)
            return ref[pl.ds(start, W + TILE), :]

        return of

    def outside(u, j):
        early = (soft_first + u + j) * TILE < W
        return jnp.where(jnp.logical_and(rank == 0, early), -1e30, 0.0)

    soft = soft_stages(
        rows, soft_q_ref, soft_ref, window(keys_ext), window(values_ext), masks, outside
    )

    key_features = dot_nn(k_ref[...], map_ref[...]).astype(BF)
    tok = lax.broadcasted_iota(jnp.int32, (TILE, TILE), 0)
    carried = state[...]
    starts, features, inner = [], {}, {}
    for t in range(tiles):
        tl = slice(t * TILE, (t + 1) * TILE)
        starts.append(carried.astype(BF))
        carried = carried + dot_tn(key_features[tl, :], v_ref[tl, :])
    state[...] = carried

    def widen(t):
        sl = slice(t * rows, (t + 1) * rows)
        qs[sl, :] = q_ref[sl, :].astype(F32)

    def feature(t):
        if t % group:
            return
        count = min(group, tiles - t)
        wide = [
            dot_nn(
                qs[pl.ds(t * rows + h, count * TILE, stride=heads), :].astype(BF), qmap_ref[h]
            ).astype(BF)
            for h in range(heads)
        ]
        for u in range(count):
            features[t + u] = jnp.concatenate([x[u * TILE : (u + 1) * TILE, :] for x in wide], 0)

    def score(t):
        inner[t] = dot_nt(features[t], key_features[t * TILE : (t + 1) * TILE, :]).astype(BF) * keep[...]

    def combine(t):
        out = dot_nn(
            jnp.concatenate([inner.pop(t), features.pop(t)], 1),
            jnp.concatenate([v_ref[t * TILE : (t + 1) * TILE, :], starts[t]], 0),
        )
        factor = lax.rsqrt((tok + (first + t * TILE + 1)).astype(F32))
        for h in range(heads):
            os[pl.ds(t * rows + h, TILE, stride=heads), :] = out[h * TILE : (h + 1) * TILE, :] * factor

    def narrow(t):
        sl = slice(t * rows, (t + 1) * rows)
        o_ref[sl, :] = os[sl, :].astype(BF)

    apart = max(1, tiles // soft_tiles)
    group = min(GROUP, tiles)

    def softmax_of(depth):
        def stage(t):
            if t % apart == 0 and t // apart < soft_tiles:
                soft[depth](t // apart)

        return stage

    def nothing(t):
        pass

    breadth(
        tiles,
        lambda t: (softmax_of(0)(t), widen(t)),
        *[lambda t: None] * (group - 1),
        feature,
        lambda t: (softmax_of(1)(t), score(t)),
        combine,
        lambda t: (softmax_of(2)(t), narrow(t)),
    )


def per_device(ranks, queries, keys, values, query_maps, key_map, linear_cotangent):
    tokens, heads, head_dim = queries.shape
    tile_rows = TILE * heads
    slab = head_dim // ranks * heads
    params = pltpu.CompilerParams(vmem_limit_bytes=VMEM_LIMIT)
    q_rows = queries.reshape(tokens * heads, head_dim)
    c_rows = linear_cotangent.reshape(tokens * heads, head_dim)

    def split(chunk):
        chunk = chunk if tokens % chunk == 0 else W
        rows = pl.BlockSpec((chunk * heads, head_dim), lambda i: (i, 0))
        return chunk, tokens // chunk, chunk * heads, rows, pl.BlockSpec((chunk, head_dim), lambda i: (i, 0))

    def whole(shape):
        return pl.BlockSpec(shape, lambda i: (0,) * len(shape))

    length = head_dim + 2 * padded16(slab)
    packets = [(length + 2 * W if k == 1 else length, head_dim) for k in range(ranks)]
    chunk, steps, chunk_rows, row_spec, key_spec = split(CHUNKS[0])
    send = pl.pallas_call(
        functools.partial(backward_kernel, heads, ranks, slab),
        grid=(steps,),
        in_specs=[row_spec, row_spec, key_spec, key_spec, whole(key_map.shape)],
        out_specs=[whole(packet) for packet in packets],
        out_shape=[jax.ShapeDtypeStruct(packet, BF) for packet in packets],
        scratch_shapes=[
            pltpu.VMEM((heads, head_dim, 2 * head_dim), F32),
            pltpu.VMEM((head_dim, head_dim), F32),
            pltpu.VMEM((tile_rows, TILE), BF),
            pltpu.VMEM((chunk_rows, head_dim), F32),
            pltpu.VMEM((chunk_rows, head_dim), F32),
            pltpu.VMEM((heads * head_dim, head_dim), F32),
            pltpu.VMEM((heads * head_dim, head_dim), F32),
        ],
        compiler_params=params,
        name="backward",
    )(q_rows, c_rows, keys, values, key_map)

    got = [
        lax.ppermute(part, "seq", [(r, (r + k) % ranks) for r in range(ranks)]) if k else part
        for k, part in enumerate(send)
    ]

    tiles = (tokens - W) // TILE
    cuts = [t for t in CUTS if t < tiles]
    masks = [pltpu.VMEM((tile_rows, TILE), kind) for kind in (F32, BF, BF)]
    in_hbm = pl.BlockSpec(memory_space=pl.ANY)
    soft_rows = pl.pallas_call(
        functools.partial(softmax_kernel, heads, cuts),
        in_specs=[in_hbm] * 3,
        out_specs=in_hbm,
        out_shape=jax.ShapeDtypeStruct(q_rows.shape, BF),
        scratch_shapes=[
            *masks,
            pltpu.VMEM((tiles * tile_rows, head_dim), BF),
            pltpu.VMEM(keys.shape, BF),
            pltpu.VMEM(keys.shape, BF),
            pltpu.VMEM((tiles * tile_rows, head_dim), BF),
            pltpu.SemaphoreType.DMA((3, len(cuts))),
            pltpu.SemaphoreType.DMA((tiles,)),
        ],
        compiler_params=params,
        name="softmax",
    )(q_rows, keys, values)

    chunk, steps, chunk_rows, row_spec, key_spec = split(CHUNKS[1])
    soft_steps = max(n for n in (1, 2, 4) if n <= steps)
    soft_spec = pl.BlockSpec(
        (W // soft_steps * heads, head_dim), lambda i: (jnp.minimum(i, soft_steps - 1), 0)
    )
    in_vmem = pl.BlockSpec(memory_space=pltpu.VMEM)
    linear_rows, soft_rows, gradient = pl.pallas_call(
        functools.partial(forward_kernel, heads, ranks, slab, soft_steps),
        grid=(steps,),
        in_specs=[
            row_spec,
            key_spec,
            key_spec,
            whole(key_map.shape),
            whole(query_maps.shape),
            soft_spec,
            *[whole(packet) for packet in packets],
            pl.BlockSpec(memory_space=pl.ANY),
        ],
        out_specs=[row_spec, soft_spec, whole((slab, head_dim))],
        out_shape=[
            jax.ShapeDtypeStruct(q_rows.shape, BF),
            jax.ShapeDtypeStruct(q_rows.shape, BF),
            jax.ShapeDtypeStruct((slab, head_dim), F32),
        ],
        scratch_shapes=[
            pltpu.VMEM((head_dim, head_dim), F32),
            pltpu.VMEM((tile_rows, TILE), BF),
            pltpu.VMEM((chunk_rows, head_dim), F32),
            pltpu.VMEM((chunk_rows, head_dim), F32),
            pltpu.VMEM((ranks, length, head_dim), BF),
            pltpu.VMEM((2 * W, head_dim), BF),
            pltpu.VMEM((2 * W, head_dim), BF),
            *masks,
        ],
        input_output_aliases={6 + ranks: 1},
        compiler_params=params,
        name="forward",
    )(q_rows, keys, values, key_map, query_maps, q_rows, *got, soft_rows)

    return (
        soft_rows.reshape(queries.shape),
        linear_rows.reshape(queries.shape),
        gradient.reshape(head_dim // ranks, heads, head_dim),
    )


def solution(mesh):
    return jax.shard_map(
        functools.partial(per_device, mesh.shape["seq"]),
        mesh=mesh,
        in_specs=(
            P(("groups", "seq"), ("head", "rep"), None),
            P(("groups", "seq"), None),
            P(("groups", "seq"), None),
            P(("groups", "head", "rep"), None, None),
            P("groups", None),
            P(("groups", "seq"), ("head", "rep"), None),
        ),
        out_specs=(
            P(("groups", "seq"), ("head", "rep"), None),
            P(("groups", "seq"), ("head", "rep"), None),
            P(("groups", "seq"), ("head", "rep"), None),
        ),
        check_vma=False,
    )
```
